32 devices in a mesh: kv: 16 (over z, x, core), tp: 2 (over y).
Axes of the slice: x: 2, y: 2, z: 4, core: 2. Of those that a mesh axis runs over, the one named last changes fastest.
Arguments:
- queries: bfloat16 [128, 7168], P('kv', 'tp'), may hold values from -30 to 30
- new_keys: bfloat16 [128, 7168], P('kv', 'tp'), may hold values from -6 to 6
- new_values: bfloat16 [128, 7168], P('kv', 'tp'), may hold values from -6 to 6
- keys: bfloat16 [6144, 7168], P('kv', 'tp'), may hold values from -8 to 8
- values: bfloat16 [6144, 7168], P('kv', 'tp'), may hold values from -6 to 6
- slot_request: int32 [6144], P('kv'), may hold values from 0 to 127, as said below
- slot_valid: int32 [6144], P('kv'), may hold values from 0 to 1, as said below
- out_weight: bfloat16 [7168, 7168], P('tp', 'kv'), may hold values from -0.0625 to 0.0625
- out_bias: bfloat16 [7168], P('kv'), may hold values from -3 to 3
- residual: bfloat16 [128, 7168], P('tp', 'kv'), may hold values from -6 to 6
Outputs:
- layer_out: bfloat16 [128, 7168], P('tp', 'kv')
The draws below stay inside these ranges and needn't reach their ends.
Inputs may be any that keep to these rules, and one draw needn't show every extreme that they name: `slot_request`: slots come in pages of 16 consecutive slots owned by one request; a request's pages are consecutive and may span several holders; every request owns at least one page and at most 130 pages, and one request owns exactly 130. `slot_valid`: only the last page of each request has empty slots, and that page holds at least one cached token in its first slot.
All inputs are finite; a program needn't handle non-finite values.
Results may differ from the reference program's by a relative error of at most 0.0033.
Values may be sent and summed in bfloat16 or wider, within the bound.
No kernel may reach another device: no remote copies, remote signals or barrier semaphores. Data moves between devices by JAX's collectives and lax.ppermute only.
A program may use at most 64 MiB of HBM per device.

```python
import math
import jax
import jax.numpy as jnp
from jax import lax

D = 7168
HEADS = 56
HD = 128
PAGE = 16
REQS = 128
PAGES = 384
SLOTS_DEV = 384
SLOTS = 6144
MAXPAGES = 130
N_KV = 16


def layout(key):
    base = jax.random.fold_in(key, 11)
    key_long, key_owner, key_order, key_fill = jax.random.split(base, 4)
    spare = PAGES - REQS - (MAXPAGES - 1)
    request_ids = jnp.arange(REQS, dtype=jnp.int32)
    long_request = jax.random.randint(key_long, (), 0, REQS, dtype=jnp.int32)
    owners = jax.random.randint(key_owner, (spare,), 0, REQS - 1, dtype=jnp.int32)
    owners = owners + (owners >= long_request).astype(jnp.int32)
    extra = jnp.sum((owners[:, None] == request_ids[None, :]).astype(jnp.int32), axis=0)
    counts = 1 + extra + (MAXPAGES - 1) * (request_ids == long_request).astype(jnp.int32)
    order = jax.random.permutation(key_order, REQS).astype(jnp.int32)
    ends = jnp.cumsum(counts[order]).astype(jnp.int32)
    page_ids = jnp.arange(PAGES, dtype=jnp.int32)
    position = jnp.sum((page_ids[:, None] >= ends[None, :]).astype(jnp.int32), axis=1)
    page_request = order[position]
    last_page = page_ids == ends[position] - 1
    fill = jax.random.randint(key_fill, (REQS,), 1, PAGE + 1, dtype=jnp.int32)
    slot_ids = jnp.arange(SLOTS, dtype=jnp.int32)
    slot_page = slot_ids // PAGE
    within = slot_ids % PAGE
    slot_owner = page_request[slot_page]
    empty = jnp.logical_and(last_page[slot_page], within >= fill[slot_owner])
    slot_live = jnp.where(empty, 0, 1).astype(jnp.int32)
    return (slot_owner.astype(jnp.int32), slot_live)


def draw_slot_request(key, part):
    slot_owner, slot_live = layout(key)
    return slot_owner


def draw_slot_valid(key, part):
    slot_owner, slot_live = layout(key)
    return slot_live


def draw_queries(key, part):
    noise_key = jax.random.fold_in(key, 31)
    noise = jnp.clip(jax.random.normal(noise_key, (REQS, D), jnp.float32), -6.0, 6.0)
    drawn = noise
    return jnp.clip(drawn, -30.0, 30.0).astype(jnp.bfloat16)


def draw_keys(key, part):
    noise_key = jax.random.fold_in(key, 51)
    noise = jnp.clip(jax.random.normal(noise_key, (SLOTS, D), jnp.float32), -6.0, 6.0)
    drawn = noise
    return jnp.clip(drawn, -8.0, 8.0).astype(jnp.bfloat16)


def level_of(stream_key, shape, cuts, low, largest):
    gain = 1.0
    for axis_at, parts in cuts:
        draws = jax.random.uniform(jax.random.fold_in(jax.random.fold_in(stream_key, 6), axis_at), (parts,), jnp.float32, low / len(cuts), largest / len(cuts))
        gain = gain * jnp.repeat(jnp.exp(draws), shape[axis_at] // parts).reshape((-1,) + (1,) * (len(shape) - 1 - axis_at))
    return gain


def normal_values(own_key, extent, width, bound, cuts=(), held_as=jnp.bfloat16):
    values = width * jax.random.normal(own_key, extent, jnp.float32)
    if cuts:
        values = values * level_of(own_key, extent, cuts, -0.22, 0.18)
    return jnp.clip(values, -bound, bound).astype(held_as)


def setup_inputs(seed: int = 0) -> dict:
    arg_keys = jax.random.split(jax.random.key(seed), 11)
    queries = draw_queries(jax.random.fold_in(arg_keys[10], 71), 0)
    new_keys = normal_values(arg_keys[1], (REQS, D), 1.0, 6.0, ((0, 16), (1, 2)))
    new_values = normal_values(arg_keys[2], (REQS, D), 1.0, 6.0, ((0, 16), (1, 2)))
    keys = draw_keys(jax.random.fold_in(arg_keys[10], 71), 0)
    values = normal_values(arg_keys[4], (SLOTS, D), 1.0, 6.0, ((0, 16), (1, 2)))
    slot_request = draw_slot_request(jax.random.fold_in(arg_keys[10], 71), 0)
    slot_valid = draw_slot_valid(jax.random.fold_in(arg_keys[10], 71), 0)
    out_weight = normal_values(arg_keys[7], (D, D), D ** -0.5, 0.0625, ((0, 2), (1, 16)))
    out_bias = normal_values(arg_keys[8], (D,), 0.5, 3.0, ((0, 16),))
    residual = normal_values(arg_keys[9], (REQS, D), 1.0, 6.0, ((0, 2), (1, 16)))
    return dict(queries=queries, new_keys=new_keys, new_values=new_values, keys=keys, values=values, slot_request=slot_request, slot_valid=slot_valid, out_weight=out_weight, out_bias=out_bias, residual=residual)


floor_score = -1e+30

def settle(x):
    return lax.optimization_barrier(x.astype(jnp.bfloat16)).astype(jnp.float32)

def reference(queries, new_keys, new_values, keys, values, slot_request, slot_valid, out_weight, out_bias, residual):
    score_scale = 1.0 / math.sqrt(HD)
    query_heads = queries.astype(jnp.float32).reshape(REQS, HEADS, HD)
    self_scores = lax.optimization_barrier(jnp.sum(query_heads * new_keys.astype(jnp.float32).reshape(REQS, HEADS, HD), axis=-1)) * score_scale
    key_blocks = keys.reshape(N_KV, SLOTS_DEV, D)
    value_blocks = values.reshape(N_KV, SLOTS_DEV, D)
    request_blocks = slot_request.reshape(N_KV, SLOTS_DEV).astype(jnp.int32)
    valid_blocks = slot_valid.reshape(N_KV, SLOTS_DEV)

    def block_scores(key_block, request_block, valid_block):
        picked = query_heads[request_block]
        scores = lax.optimization_barrier(jnp.sum(picked * key_block.astype(jnp.float32).reshape(SLOTS_DEV, HEADS, HD), axis=-1)) * score_scale
        return jnp.where((valid_block == 1)[:, None], scores, floor_score)

    def max_step(row_top, blocks):
        key_block, value_block, request_block, valid_block = blocks
        scores = block_scores(key_block, request_block, valid_block)
        return (row_top.at[request_block].max(scores), None)
    row_top, _ = lax.scan(max_step, self_scores, (key_blocks, value_blocks, request_blocks, valid_blocks))
    self_weight = settle(jnp.exp(self_scores - row_top))
    numer_start = self_weight[:, :, None] * new_values.astype(jnp.float32).reshape(REQS, HEADS, HD)

    def sum_step(carry, blocks):
        numer, denom = carry
        key_block, value_block, request_block, valid_block = blocks
        scores = block_scores(key_block, request_block, valid_block)
        weights = settle(jnp.where((valid_block == 1)[:, None], jnp.exp(scores - row_top[request_block]), 0.0))
        weighted = weights[:, :, None] * value_block.astype(jnp.float32).reshape(SLOTS_DEV, HEADS, HD)
        numer = numer + jax.ops.segment_sum(weighted, request_block, num_segments=REQS)
        denom = denom + jax.ops.segment_sum(weights, request_block, num_segments=REQS)
        return ((numer, denom), None)
    (numer, denom), _ = lax.scan(sum_step, (numer_start, self_weight), (key_blocks, value_blocks, request_blocks, valid_blocks))
    attended = (numer / denom[:, :, None]).reshape(REQS, D).astype(jnp.bfloat16)
    projected = jnp.dot(attended, out_weight, preferred_element_type=jnp.float32)
    total = residual.astype(jnp.float32) + projected + out_bias.astype(jnp.float32)[None, :]
    return total.astype(jnp.bfloat16)
```

```python
import functools
import math

import jax
import jax.numpy as jnp
from jax import lax
from jax.experimental import pallas as pl
from jax.experimental.pallas import tpu as pltpu
from jax.sharding import PartitionSpec as P

HD = 128
PAGE = 16
OUTER = 4
LANES = 128
STAT = 32

floor_score = -1e30
f32 = jnp.float32
bf16 = jnp.bfloat16
WHOLE = pl.BlockSpec(memory_space=pltpu.VMEM)
SCALARS = pl.BlockSpec(memory_space=pltpu.SMEM)


def params(megabytes=48):
    return pltpu.CompilerParams(vmem_limit_bytes=megabytes * 1024 * 1024)


def offset_of(block, mid):
    core = block // (mid * OUTER)
    middle = (block // OUTER) % mid
    return core + 2 * middle + 2 * mid * (block % OUTER)


def place_of(offset, mid):
    core = offset % 2
    middle = (offset // 2) % mid
    return (core * mid + middle) * OUTER + offset // (2 * mid)


def prep_kernel(mid, own_rows, ids, request, valid, queries, new_keys, pick, mask, own_top):
    rows, slots = mask.shape
    row = lax.broadcasted_iota(jnp.int32, (rows, slots), 0)
    lane = lax.broadcasted_iota(jnp.int32, (rows, slots), 1)
    owners = jnp.broadcast_to(request[...], (rows, slots))
    mine = jnp.sum(jnp.where(lane == row * PAGE, owners, 0), axis=1, keepdims=True)
    before = jnp.sum(jnp.where(lane == row * PAGE - PAGE, owners, 0), axis=1, keepdims=True)
    page = lax.broadcasted_iota(jnp.int32, (rows, 1), 0)
    first = ((page == 0) | (mine != before)) & (page < slots // PAGE)
    live = (owners == mine) & first & (jnp.broadcast_to(valid[...], (rows, slots)) == 1)
    mask[...] = jnp.where(live, 1.0, 0.0)
    place = lax.broadcasted_iota(jnp.int32, pick.shape, 1)
    owner = lax.bitwise_xor(offset_of(place // own_rows, mid), ids[0])
    named = owner * own_rows + place % own_rows
    pick[...] = jnp.where((named == mine) & first, 1.0, 0.0).astype(bf16)
    heads = queries.shape[1] // HD
    where = lax.broadcasted_iota(jnp.int32, own_top.shape, 1)
    top = jnp.zeros(own_top.shape, f32)
    for head in range(heads):
        cut = slice(head * HD, (head + 1) * HD)
        score = jnp.sum(
            queries[:, cut].astype(f32) * new_keys[:, cut].astype(f32), axis=1, keepdims=True
        ) * (1.0 / math.sqrt(HD))
        top = jnp.where(where == head, score, top)
    own_top[...] = top


def split_top(top):
    lane = lax.broadcasted_iota(jnp.int32, top.shape, 1)
    top = jnp.where(lane < STAT, top, 0.0)
    high = top.astype(bf16).astype(f32)
    rest = top - high
    middle = rest.astype(bf16).astype(f32)
    low = rest - middle
    return high + pltpu.roll(middle, STAT, 1) + pltpu.roll(low, 2 * STAT, 1)


def join_top(stat):
    return (stat + pltpu.roll(stat, LANES - STAT, 1)) + pltpu.roll(stat, LANES - 2 * STAT, 1)


def attend_kernel(group, pick, mask, near, far, keys, values, keep, send, tops):
    step = pl.program_id(0)
    rows = pick.shape[0]
    half = near.shape[0]
    total = 2 * half
    chosen = jnp.dot(
        pick[:, :half], near[...], preferred_element_type=f32
    ) + jnp.dot(pick[:, half:], far[...], preferred_element_type=f32)
    chosen = chosen.astype(bf16)
    live = mask[...] > 0.0
    lane = lax.broadcasted_iota(jnp.int32, (rows, LANES), 1)

    @pl.when(step == 0)
    def _():
        tops[...] = jnp.zeros_like(tops)

    top_all = tops[...]
    found = []
    for head in range(group):
        cut = slice(head * HD, (head + 1) * HD)
        score = lax.dot_general(
            chosen[:, cut], keys[:, cut], (((1,), (1,)), ((), ())), preferred_element_type=f32
        ) * (1.0 / math.sqrt(HD))
        score = jnp.where(live, score, floor_score)
        top = jnp.max(score, axis=1, keepdims=True)
        weight = jnp.where(live, jnp.exp(score - top), 0.0).astype(bf16)
        denom = jnp.sum(weight.astype(f32), axis=1, keepdims=True)
        denom = jnp.where(denom > 0.0, denom, 1.0)
        numer = jnp.dot(weight, values[:, cut], preferred_element_type=f32)
        found.append((numer / denom).astype(bf16))
        top_all = jnp.where(lane == step * group + head, top + jnp.log(denom), top_all)
    tops[...] = top_all
    spread = functools.partial(
        lax.dot_general, dimension_numbers=(((0,), (0,)), ((), ())), preferred_element_type=f32
    )
    dense = spread(pick[...], jnp.concatenate(found, axis=1)).astype(bf16)
    columns = pl.ds(pl.multiple_of(step * group * HD, HD), group * HD)
    keep[:, columns] = dense[:half]
    send[:, columns] = dense[half:]

    @pl.when(step == pl.num_programs(0) - 1)
    def _():
        stat = jnp.where(lane == LANES - 1, 1.0, split_top(tops[...])).astype(bf16)
        wide = spread(pick[...], stat)
        place = lax.broadcasted_iota(jnp.int32, (total, LANES), 1)
        absent = wide[:, LANES - 1 :] == 0.0
        wide = jnp.where(absent & (place < STAT), floor_score, wide).astype(bf16)
        start = keep.shape[1] - LANES
        keep[:, start:] = wide[:half]
        send[:, start:] = wide[half:]


def merge(parts, tops):
    best = functools.reduce(jnp.maximum, tops)
    weights = [jnp.exp(top - best) for top in tops]
    total = functools.reduce(jnp.add, weights)
    shares = [weight / total for weight in weights]

    def head_of(head):
        terms = [
            share[:, head : head + 1] * part(head) for share, part in zip(shares, parts)
        ]
        return functools.reduce(jnp.add, terms)

    return head_of, best + jnp.log(total)


def part_of(ref):
    return lambda head: ref[:, head * HD : (head + 1) * HD].astype(f32)


def top_of(ref):
    return join_top(ref[:, ref.shape[1] - LANES :].astype(f32))


def merge_kernel(count, *refs):
    ins, outs = refs[:count], refs[count:]
    heads = ins[0].shape[1] // HD - 1
    rows = outs[0].shape[0]
    head_of, top = merge([part_of(ref) for ref in ins], [top_of(ref) for ref in ins])
    for head in range(heads + 1):
        cut = slice(head * HD, (head + 1) * HD)
        block = head_of(head) if head < heads else split_top(top)
        for at, out in enumerate(outs):
            out[:, cut] = block[at * rows : (at + 1) * rows].astype(bf16)


def last_kernel(count, *refs):
    ins = refs[:count]
    new_values, own_top, out = refs[count:]
    head_of, _ = merge(
        [part_of(ref) for ref in ins] + [part_of(new_values)],
        [top_of(ref) for ref in ins] + [own_top[...]],
    )
    for head in range(out.shape[1] // HD):
        out[:, head * HD : (head + 1) * HD] = head_of(head).astype(bf16)


def project_kernel(mid, own_rows, ids, *refs):
    count = len(refs) - 1
    acc = refs[-1]
    places = [at for at in range(count) if refs[at].dtype == f32]
    ins, weight, outs = refs[: places[0] - 1], refs[places[0] - 1], refs[places[0] : count]
    step = pl.program_id(0)

    @pl.when(step == 0)
    def _():
        acc[...] = jnp.zeros_like(acc)

    at = 0
    for ref in ins:
        rows = ref.shape[0]
        acc[at : at + rows, :] += jnp.dot(ref[...], weight[...], preferred_element_type=f32)
        at += rows

    @pl.when(step == pl.num_programs(0) - 1)
    def _():
        blocks = outs[0].shape[0] // own_rows
        for distance, out in enumerate(outs):
            side = lax.bitwise_xor(ids[1], distance)
            for block in range(blocks):
                offset = lax.bitwise_xor(side * blocks + block, ids[0])
                start = pl.multiple_of(place_of(offset, mid) * own_rows, own_rows)
                out[block * own_rows : (block + 1) * own_rows, :] = acc[pl.ds(start, own_rows), :]


def hop(x, axis, count, distance):
    return lax.ppermute(x, axis, [(i, i ^ distance) for i in range(count)])


def on_device(
    kv_count,
    tp_count,
    queries,
    new_keys,
    new_values,
    keys,
    values,
    slot_request,
    slot_valid,
    out_weight,
    out_bias,
    residual,
):
    own_rows, width = queries.shape
    heads = width // HD
    slots = keys.shape[0]
    mid = kv_count // (2 * OUTER)
    requests = kv_count * own_rows
    rows = -(-(slots // PAGE) // 16) * 16
    group = 7 if heads % 7 == 0 else 1
    columns = out_weight.shape[1]
    wide = width + LANES
    ids = jnp.stack([lax.axis_index("kv"), lax.axis_index("tp")]).astype(jnp.int32)
    kv_hop = lambda x, distance: hop(x, "kv", kv_count, distance)

    def gather(block):
        line = jnp.concatenate(
            [block] + [kv_hop(block, 2 * mid * far) for far in range(1, OUTER)], axis=0
        )
        lines = [line] + [kv_hop(line, 2 * near) for near in range(1, mid)]
        return lines, [kv_hop(each, 1) for each in lines]

    pick, mask, own_top = pl.pallas_call(
        functools.partial(prep_kernel, mid, own_rows),
        out_shape=(
            jax.ShapeDtypeStruct((rows, requests), bf16),
            jax.ShapeDtypeStruct((rows, slots), f32),
            jax.ShapeDtypeStruct((own_rows, LANES), f32),
        ),
        in_specs=[SCALARS] + [WHOLE] * 4,
        out_specs=(WHOLE,) * 3,
        compiler_params=params(),
        name="prep",
    )(ids, slot_request.reshape(1, slots), slot_valid.reshape(1, slots), queries, new_keys)

    near, far = gather(queries)
    near = jnp.concatenate(near, axis=0)
    far = jnp.concatenate(far, axis=0)
    half = requests // 2
    fixed = lambda shape: pl.BlockSpec(shape, lambda step: (0, 0))
    moving = lambda height: pl.BlockSpec((height, group * HD), lambda step: (0, step))
    keep, send = pl.pallas_call(
        functools.partial(attend_kernel, group),
        grid=(heads // group,),
        out_shape=(jax.ShapeDtypeStruct((half, wide), bf16),) * 2,
        in_specs=[
            fixed((rows, requests)),
            fixed((rows, slots)),
            moving(half),
            moving(half),
            moving(slots),
            moving(slots),
        ],
        out_specs=(fixed((half, wide)),) * 2,
        scratch_shapes=[pltpu.VMEM((rows, LANES), f32)],
        compiler_params=params(),
        name="attend",
    )(pick, mask, near, far, keys, values)

    def merged(ins, count):
        size = ins[0].shape[0] // count
        return pl.pallas_call(
            functools.partial(merge_kernel, len(ins)),
            out_shape=(jax.ShapeDtypeStruct((size, wide), bf16),) * count,
            in_specs=[WHOLE] * len(ins),
            out_specs=(WHOLE,) * count,
            compiler_params=params(),
            name="merge",
        )(*ins)

    blocks = merged([keep, kv_hop(send, 1)], mid)
    blocks = merged(
        [blocks[0]] + [kv_hop(blocks[near], 2 * near) for near in range(1, mid)], OUTER
    )
    ins = [blocks[0]] + [kv_hop(blocks[far], 2 * mid * far) for far in range(1, OUTER)]
    attended = pl.pallas_call(
        functools.partial(last_kernel, len(ins)),
        out_shape=jax.ShapeDtypeStruct((own_rows, width), bf16),
        in_specs=[WHOLE] * (len(ins) + 2),
        out_specs=WHOLE,
        compiler_params=params(),
        name="last",
    )(*ins, new_values, own_top)

    near, far = gather(attended)
    tall = requests // tp_count
    deep = 4 if heads % 4 == 0 else 7 if heads % 7 == 0 else 1
    ins = near + far
    outs = project(ids, ins, out_weight, mid, own_rows, deep, tall)
    total = outs[0]
    for distance in range(1, tp_count):
        total = total + hop(outs[distance], "tp", tp_count, distance)
    total = total + residual.astype(f32) + out_bias.astype(f32)[None, :]
    return total.astype(bf16)


def project(ids, ins, out_weight, mid, own_rows, deep, tall):
    columns = out_weight.shape[1]
    depth = out_weight.shape[0]
    requests = sum(each.shape[0] for each in ins)
    return pl.pallas_call(
        functools.partial(project_kernel, mid, own_rows),
        grid=(depth // (deep * HD),),
        out_shape=(jax.ShapeDtypeStruct((tall, columns), f32),) * (requests // tall),
        in_specs=[SCALARS]
        + [pl.BlockSpec((each.shape[0], deep * HD), lambda step: (0, step)) for each in ins]
        + [pl.BlockSpec((deep * HD, columns), lambda step: (step, 0))],
        out_specs=(pl.BlockSpec((tall, columns), lambda step: (0, 0)),) * (requests // tall),
        scratch_shapes=[pltpu.VMEM((requests, columns), f32)],
        compiler_params=params(),
        name="project",
    )(ids, *ins, out_weight)


def solution(mesh):
    placed = (
        P("kv", "tp"),
        P("kv", "tp"),
        P("kv", "tp"),
        P("kv", "tp"),
        P("kv", "tp"),
        P("kv"),
        P("kv"),
        P("tp", "kv"),
        P("kv"),
        P("tp", "kv"),
    )
    return jax.shard_map(
        functools.partial(on_device, mesh.shape["kv"], mesh.shape["tp"]),
        mesh=mesh,
        in_specs=placed,
        out_specs=P("tp", "kv"),
        check_vma=False,
    )
```

```python
import functools
import math

import jax
import jax.numpy as jnp
from jax import lax
from jax.experimental import pallas as pl
from jax.experimental.pallas import tpu as pltpu
from jax.sharding import PartitionSpec as P

HD = 128
PAGE = 16
OUTER = 4
LANES = 128
STAT = 32

floor_score = -1e30
PACK_US = 5
f32 = jnp.float32
bf16 = jnp.bfloat16
WHOLE = pl.BlockSpec(memory_space=pltpu.VMEM)
SCALARS = pl.BlockSpec(memory_space=pltpu.SMEM)
ANY = pl.BlockSpec(memory_space=pl.ANY)


def params(megabytes=24):
    return pltpu.CompilerParams(vmem_limit_bytes=megabytes * 1024 * 1024)


def offset_of(block, mid):
    core = block // (mid * OUTER)
    middle = (block // OUTER) % mid
    return core + 2 * middle + 2 * mid * (OUTER - 1 - block % OUTER)


def place_of(offset, mid):
    core = offset % 2
    middle = (offset // 2) % mid
    return (core * mid + middle) * OUTER + OUTER - 1 - offset // (2 * mid)


def prep_kernel(
    mid, own_rows, ids, request, valid, queries, new_keys, pick, mask, own_top
):
    rows, slots = mask.shape
    row = lax.broadcasted_iota(jnp.int32, (rows, slots), 0)
    lane = lax.broadcasted_iota(jnp.int32, (rows, slots), 1)
    owners = jnp.broadcast_to(request[...], (rows, slots))
    mine = jnp.sum(jnp.where(lane == row * PAGE, owners, 0), axis=1, keepdims=True)
    before = jnp.sum(jnp.where(lane == row * PAGE - PAGE, owners, 0), axis=1, keepdims=True)
    page = lax.broadcasted_iota(jnp.int32, (rows, 1), 0)
    first = ((page == 0) | (mine != before)) & (page < slots // PAGE)
    live = (owners == mine) & first & (jnp.broadcast_to(valid[...], (rows, slots)) == 1)
    mask[...] = jnp.where(live, 1.0, 0.0)
    place = lax.broadcasted_iota(jnp.int32, pick.shape, 1)
    owner = lax.bitwise_xor(offset_of(place // own_rows, mid), ids[0])
    named = owner * own_rows + place % own_rows
    pick[...] = jnp.where((named == mine) & first, 1.0, 0.0).astype(bf16)
    heads = queries.shape[1] // HD
    where = lax.broadcasted_iota(jnp.int32, own_top.shape, 1)
    top = jnp.zeros(own_top.shape, f32)
    for head in range(heads):
        cut = slice(head * HD, (head + 1) * HD)
        score = jnp.sum(
            queries[:, cut].astype(f32) * new_keys[:, cut].astype(f32), axis=1, keepdims=True
        ) * (1.0 / math.sqrt(HD))
        top = jnp.where(where == head, score, top)
    own_top[...] = top


def split_top(top):
    lane = lax.broadcasted_iota(jnp.int32, top.shape, 1)
    top = jnp.where(lane < STAT, top, 0.0)
    high = top.astype(bf16).astype(f32)
    rest = top - high
    middle = rest.astype(bf16).astype(f32)
    low = rest - middle
    return high + pltpu.roll(middle, STAT, 1) + pltpu.roll(low, 2 * STAT, 1)


def join_top(stat):
    return (stat + pltpu.roll(stat, LANES - STAT, 1)) + pltpu.roll(stat, LANES - 2 * STAT, 1)


def stacked(refs):
    return jnp.concatenate([ref[...].astype(f32) for ref in refs], axis=0)


def pack_kernel(count, tail, *refs):
    outs = refs[len(refs) - 1 - tail :]
    rows = stacked(refs[:count]).astype(bf16)
    outs[0][...] = rows
    if tail:
        outs[1][...] = rows[: outs[1].shape[0]]


def attend_kernel(count, pick, mask, keys, values, *refs):
    blocks, (keep, send) = refs[:count], refs[count:]
    rows = pick.shape[0]
    heads = keys.shape[1] // HD
    half = keep.shape[0]
    lane = lax.broadcasted_iota(jnp.int32, (rows, LANES), 1)
    live = mask[...] > 0.0
    chosen = jnp.dot(pick[...], stacked(blocks).astype(bf16), preferred_element_type=f32)
    zero = jnp.zeros((rows, HD), f32)
    sets = [tuple(range(at, min(at + 2, heads))) for at in range(0, heads, 2)]
    cuts = [slice(each[0] * HD, (each[-1] + 1) * HD) for each in sets]

    def diagonal(each):
        bands = [
            jnp.concatenate(
                [chosen[:, head * HD : (head + 1) * HD] if other == head else zero for other in each],
                axis=1,
            )
            for head in each
        ]
        return jnp.concatenate(bands, axis=0).astype(bf16)

    scores = [
        lax.dot_general(
            diagonal(each), keys[:, cut], (((1,), (1,)), ((), ())), preferred_element_type=f32
        )
        for each, cut in zip(sets, cuts)
    ]
    tops = jnp.zeros((rows, LANES), f32)
    weights, denoms = [], []
    for each, score in zip(sets, scores):
        wide = jnp.concatenate([live] * len(each), axis=0)
        score = jnp.where(wide, score * (1.0 / math.sqrt(HD)), floor_score)
        top = jnp.max(score, axis=1, keepdims=True)
        weight = jnp.where(wide, jnp.exp(score - top), 0.0).astype(bf16)
        denom = jnp.sum(weight.astype(f32), axis=1, keepdims=True)
        denom = jnp.where(denom > 0.0, denom, 1.0)
        weights.append(weight)
        denoms.append(denom)
        for at, head in enumerate(each):
            part = slice(at * rows, (at + 1) * rows)
            tops = jnp.where(lane == head, top[part] + jnp.log(denom[part]), tops)
    found = []
    for each, cut, weight, denom in zip(sets, cuts, weights, denoms):
        numer = jnp.dot(weight, values[:, cut], preferred_element_type=f32) / denom
        for at in range(len(each)):
            found.append(numer[at * rows : (at + 1) * rows, at * HD : (at + 1) * HD])
    spread = functools.partial(
        lax.dot_general, dimension_numbers=(((0,), (0,)), ((), ())), preferred_element_type=f32
    )
    dense = spread(pick[...], jnp.concatenate(found, axis=1).astype(bf16)).astype(bf16)
    stat = jnp.where(lane == LANES - 1, 1.0, split_top(tops)).astype(bf16)
    stat = spread(pick[...], stat)
    place = lax.broadcasted_iota(jnp.int32, stat.shape, 1)
    absent = stat[:, LANES - 1 :] == 0.0
    stat = jnp.where(absent & (place < STAT), floor_score, stat).astype(bf16)
    for out, part in ((keep, slice(0, half)), (send, slice(half, 2 * half))):
        out[:, : heads * HD] = dense[part]
        out[:, heads * HD :] = stat[part]


def merge(parts, tops):
    best = functools.reduce(jnp.maximum, tops)
    weights = [jnp.exp(top - best) for top in tops]
    total = functools.reduce(jnp.add, weights)
    shares = [weight / total for weight in weights]

    def head_of(head):
        terms = [
            share[:, head : head + 1] * part(head) for share, part in zip(shares, parts)
        ]
        return functools.reduce(jnp.add, terms)

    return head_of, best + jnp.log(total)


def part_of(ref):
    return lambda head: ref[:, head * HD : (head + 1) * HD].astype(f32)


def top_of(ref):
    return join_top(ref[:, ref.shape[1] - LANES :].astype(f32))


def merge_kernel(count, *refs):
    ins, outs = refs[:count], refs[count:]
    heads = ins[0].shape[1] // HD - 1
    rows = outs[0].shape[0]
    head_of, top = merge([part_of(ref) for ref in ins], [top_of(ref) for ref in ins])
    for head in range(heads + 1):
        cut = slice(head * HD, (head + 1) * HD)
        block = head_of(head) if head < heads else split_top(top)
        for at, out in enumerate(outs):
            out[:, cut] = block[at * rows : (at + 1) * rows].astype(bf16)


def last_kernel(count, *refs):
    ins = refs[:count]
    new_values, own_top, out = refs[count:]
    head_of, _ = merge(
        [part_of(ref) for ref in ins] + [part_of(new_values)],
        [top_of(ref) for ref in ins] + [own_top[...]],
    )
    for head in range(out.shape[1] // HD):
        out[:, head * HD : (head + 1) * HD] = head_of(head).astype(bf16)


def by_weight(blocks, weight):
    return lax.dot_general(
        stacked(blocks).astype(bf16), weight[...], (((1,), (1,)), ((), ())), preferred_element_type=f32
    )


def project_kernel(mid, own_rows, count, ids, *refs):
    blocks, weight, outs, acc = refs[:count], refs[count], refs[count + 1 : -1], refs[-1]
    acc[...] = by_weight(blocks, weight)
    owners = outs[0].shape[0] // own_rows
    for distance, out in enumerate(outs):
        side = lax.bitwise_xor(ids[1], distance)
        for at in range(owners):
            offset = lax.bitwise_xor(side * owners + at, ids[0])
            start = pl.multiple_of(place_of(offset, mid) * own_rows, own_rows)
            out[at * own_rows : (at + 1) * own_rows, :] = acc[pl.ds(start, own_rows), :]


def part_kernel(mid, nears, own_rows, count, ids, *refs):
    blocks, weight, outs, acc = refs[:count], refs[count], refs[count + 1 : -1], refs[-1]
    acc[...] = by_weight(blocks, weight)
    outers = outs[0].shape[0] // (own_rows * 2 * len(nears))
    for distance, out in enumerate(outs):
        side = lax.bitwise_xor(ids[1], distance)
        for at in range(len(nears) * outers * 2):
            near, outer, core = at // (2 * outers), side * outers + (at // 2) % outers, at % 2
            place = lax.bitwise_xor(core, ids[0] % 2) * len(nears) + near
            place = place * OUTER + OUTER - 1 - lax.bitwise_xor(outer, ids[0] // (2 * mid))
            start = pl.multiple_of(place * own_rows, own_rows)
            out[at * own_rows : (at + 1) * own_rows, :] = acc[pl.ds(start, own_rows), :]


def add_part(total, part, mid, nears, own_rows, ids):
    outers = part.shape[0] // (own_rows * 2 * len(nears))
    for at in range(len(nears) * outers * 2):
        near, outer, core = at // (2 * outers), (at // 2) % outers, at % 2
        middle = lax.bitwise_xor((ids[0] // 2) % mid, nears[near])
        start = pl.multiple_of(((outer * mid + middle) * 2 + core) * own_rows, own_rows)
        total[pl.ds(start, own_rows), :] += part[at * own_rows : (at + 1) * own_rows]


def base_kernel(mid, own_rows, ids, kept, residual, bias, total):
    total[...] = residual[...].astype(f32) + bias[...].astype(f32)
    add_part(total, kept[...], mid, (0,), own_rows, ids)


def final_kernel(mid, nears, own_rows, ids, base, early, kept, received, out, total):
    total[...] = base[...]
    add_part(total, early[...], mid, (0,), own_rows, ids)
    add_part(total, kept[...] + received[...], mid, nears, own_rows, ids)
    out[...] = total[...].astype(bf16)


def hop(x, axis, count, distance):
    return lax.ppermute(x, axis, [(i, i ^ distance) for i in range(count)])


def on_device(
    kv_count,
    tp_count,
    queries,
    new_keys,
    new_values,
    keys,
    values,
    slot_request,
    slot_valid,
    out_weight,
    out_bias,
    residual,
):
    own_rows, width = queries.shape
    slots = keys.shape[0]
    mid = kv_count // (2 * OUTER)
    requests = kv_count * own_rows
    rows = -(-(slots // PAGE) // 16) * 16
    wide = width + LANES
    ids = jnp.stack([lax.axis_index("kv"), lax.axis_index("tp")]).astype(jnp.int32)
    kv_hop = lambda x, distance: hop(x, "kv", kv_count, distance)
    shaped = jax.ShapeDtypeStruct

    def call(kernel, shapes, scratch, name, *operands, spec=lambda at: WHOLE, us=1):
        single = not isinstance(shapes, tuple)
        return pl.pallas_call(
            kernel,
            out_shape=shapes,
            in_specs=[SCALARS if x is ids else spec(at) for at, x in enumerate(operands)],
            out_specs=WHOLE if single else (WHOLE,) * len(shapes),
            scratch_shapes=scratch,
            compiler_params=params(),
            cost_estimate=pl.CostEstimate(
                flops=0, bytes_accessed=int(us * 3.5e6), transcendentals=0
            ),
            name=name,
        )(*operands)

    def pack(parts, head, after):
        height = sum(x.shape[0] for x in parts)
        shapes = [shaped((rows, width), bf16) for rows in (height, head) if rows]
        return call(
            functools.partial(pack_kernel, len(parts), len(shapes) - 1),
            tuple(shapes),
            [],
            "pack",
            *parts,
            *after,
            spec=lambda at: WHOLE if at < len(parts) else ANY,
            us=PACK_US,
        )

    def gather(block, before, between):
        outer = {far: kv_hop(block, 2 * mid * far) for far in (3, 2, 1)}
        own = {near: kv_hop(block, 2 * near) for near in range(1, mid)}
        near_all, pair = pack([outer[3], outer[2], outer[1], block], 2 * own_rows, [*own.values(), *before])
        near_other = kv_hop(near_all, 1)
        far = []
        for near in range(1, mid):
            far += [kv_hop(pair, 2 * near), kv_hop(outer[1], 2 * near), own[near]]
        after, kept = between(near_all, near_other)
        (far_all,) = pack(far, 0, after)
        return near_all, far_all, near_other, kv_hop(far_all, 1), kept

    pick, mask, own_top = call(
        functools.partial(prep_kernel, mid, own_rows),
        (
            shaped((rows, requests), bf16),
            shaped((rows, slots), f32),
            shaped((own_rows, LANES), f32),
        ),
        [],
        "prep",
        ids,
        slot_request.reshape(1, slots),
        slot_valid.reshape(1, slots),
        queries,
        new_keys,
    )
    *blocks, _ = gather(queries, [keys], lambda near_all, near_other: ([pick, values], None))
    half = requests // 2
    keep, send = call(
        functools.partial(attend_kernel, len(blocks)),
        (shaped((half, wide), bf16),) * 2,
        [],
        "attend",
        pick,
        mask,
        keys,
        values,
        *blocks,
    )

    def merged(ins, count):
        size = ins[0].shape[0] // count
        return call(
            functools.partial(merge_kernel, len(ins)),
            (shaped((size, wide), bf16),) * count,
            [],
            "merge",
            *ins,
        )

    blocks = merged([keep, kv_hop(send, 1)], 2 * mid)
    outer = []
    for at in (0, 1):
        there = [kv_hop(blocks[2 * near + at], 2 * near) for near in range(1, mid)]
        outer += merged([blocks[at]] + there, 2)
    ins = [outer[3]] + [kv_hop(outer[OUTER - 1 - far], 2 * mid * far) for far in (3, 2, 1)]
    attended = call(
        functools.partial(last_kernel, len(ins)),
        shaped((own_rows, width), bf16),
        [],
        "last",
        *ins,
        new_values,
        own_top,
    )

    weight = out_weight.T
    columns = out_weight.shape[1]

    def projected(kernel, blocks, nears):
        height = 2 * OUTER * nears * own_rows
        return call(
            functools.partial(kernel, own_rows, len(blocks)),
            (shaped((height // tp_count, columns), f32),) * tp_count,
            [pltpu.VMEM((height, columns), f32)],
            "project",
            ids,
            *blocks,
            weight,
        )

    tp_hop = lambda x, distance: hop(x, "tp", tp_count, distance)
    sets = ((0,), tuple(range(1, mid)))
    if tp_count == 2 and (kv_count // tp_count) % (2 * mid) == 0:

        def early(near_all, near_other):
            part = functools.partial(part_kernel, mid, sets[0])
            kept, sent = projected(part, [near_all, near_other], 1)
            base = call(
                functools.partial(base_kernel, mid, own_rows),
                shaped(residual.shape, f32),
                [],
                "base",
                ids,
                kept,
                residual,
                out_bias.reshape(1, columns),
            )
            return [base], [base, tp_hop(sent, 1)]

        _, far_all, _, far_other, parts = gather(attended, [], early)
        part = functools.partial(part_kernel, mid, sets[1])
        kept, sent = projected(part, [far_all, far_other], mid - 1)
        return call(
            functools.partial(final_kernel, mid, sets[1], own_rows),
            shaped(residual.shape, bf16),
            [pltpu.VMEM(residual.shape, f32)],
            "final",
            ids,
            *parts,
            kept,
            tp_hop(sent, 1),
        )
    *blocks, _ = gather(attended, [], lambda near_all, near_other: ([], None))
    outs = projected(functools.partial(project_kernel, mid), blocks, mid)
    total = outs[0]
    for distance in range(1, tp_count):
        total = total + tp_hop(outs[distance], distance)
    total = total + residual.astype(f32) + out_bias.astype(f32)[None, :]
    return total.astype(bf16)


def solution(mesh):
    placed = (
        P("kv", "tp"),
        P("kv", "tp"),
        P("kv", "tp"),
        P("kv", "tp"),
        P("kv", "tp"),
        P("kv"),
        P("kv"),
        P("tp", "kv"),
        P("kv"),
        P("tp", "kv"),
    )
    return jax.shard_map(
        functools.partial(on_device, mesh.shape["kv"], mesh.shape["tp"]),
        mesh=mesh,
        in_specs=placed,
        out_specs=P("tp", "kv"),
        check_vma=False,
    )
```

```python
import functools
import math

import jax
import jax.numpy as jnp
from jax import lax
from jax.experimental import pallas as pl
from jax.experimental.pallas import tpu as pltpu
from jax.sharding import PartitionSpec as P

HD = 128
PAGE = 16
OUTER = 4
LANES = 128
STAT = 32

floor_score = -1e30
SENT = jnp.bfloat16
f32 = jnp.float32
bf16 = jnp.bfloat16
WHOLE = pl.BlockSpec(memory_space=pltpu.VMEM)
ANY = pl.BlockSpec(memory_space=pl.ANY)


def params(megabytes=24):
    return pltpu.CompilerParams(vmem_limit_bytes=megabytes * 1024 * 1024)


def offset_of(block, mid):
    core = block // (mid * OUTER)
    middle = (block // OUTER) % mid
    return core + 2 * middle + 2 * mid * (OUTER - 1 - block % OUTER)


def place_of(offset, mid):
    core = offset % 2
    middle = (offset // 2) % mid
    return (core * mid + middle) * OUTER + OUTER - 1 - offset // (2 * mid)


def prep_kernel(mid, own_rows, request, valid, queries, new_keys, pick, mask, own_top, held):
    rows, slots = mask.shape
    row = lax.broadcasted_iota(jnp.int32, (rows, slots), 0)
    lane = lax.broadcasted_iota(jnp.int32, (rows, slots), 1)
    owners = jnp.broadcast_to(request[...], (rows, slots))
    mine = jnp.sum(jnp.where(lane == row * PAGE, owners, 0), axis=1, keepdims=True)
    before = jnp.sum(jnp.where(lane == row * PAGE - PAGE, owners, 0), axis=1, keepdims=True)
    page = lax.broadcasted_iota(jnp.int32, (rows, 1), 0)
    first = ((page == 0) | (mine != before)) & (page < slots // PAGE)
    live = (owners == mine) & first & (jnp.broadcast_to(valid[...], (rows, slots)) == 1)
    mask[...] = jnp.where(live, 1.0, 0.0)
    place = lax.broadcasted_iota(jnp.int32, pick.shape, 1)
    owner = lax.bitwise_xor(offset_of(place // own_rows, mid), lax.axis_index("kv"))
    named = owner * own_rows + place % own_rows
    pick[...] = jnp.where((named == mine) & first, 1.0, 0.0).astype(bf16)
    heads = queries.shape[1] // HD
    where = lax.broadcasted_iota(jnp.int32, own_top.shape, 1)
    top = jnp.zeros(own_top.shape, f32)
    for head in range(heads):
        cut = slice(head * HD, (head + 1) * HD)
        score = jnp.sum(
            queries[:, cut].astype(f32) * new_keys[:, cut].astype(f32), axis=1, keepdims=True
        ) * (1.0 / math.sqrt(HD))
        top = jnp.where(where == head, score, top)
    own_top[...] = top
    held[...] = queries[...]


def split_top(top):
    lane = lax.broadcasted_iota(jnp.int32, top.shape, 1)
    top = jnp.where(lane < STAT, top, 0.0)
    high = top.astype(bf16).astype(f32)
    rest = top - high
    middle = rest.astype(bf16).astype(f32)
    low = rest - middle
    return high + pltpu.roll(middle, STAT, 1) + pltpu.roll(low, 2 * STAT, 1)


def join_top(stat):
    return (stat + pltpu.roll(stat, LANES - STAT, 1)) + pltpu.roll(stat, LANES - 2 * STAT, 1)


def stacked(refs):
    return jnp.concatenate([ref[...].astype(f32) for ref in refs], axis=0)


def pack_kernel(count, *refs):
    refs[-1][...] = stacked(refs[:count]).astype(bf16)


def ready_kernel(*refs):
    refs[-1][...] = jnp.zeros_like(refs[-1])


def attend_kernel(count, pick, mask, keys, values, *refs):
    blocks, (keep, send) = refs[:count], refs[count:]
    rows = pick.shape[0]
    heads = keys.shape[1] // HD
    half = keep.shape[0]
    lane = lax.broadcasted_iota(jnp.int32, (rows, LANES), 1)
    live = mask[...] > 0.0
    chosen = jnp.dot(pick[...], stacked(blocks).astype(bf16), preferred_element_type=f32)
    zero = jnp.zeros((rows, HD), f32)
    sets = [tuple(range(at, min(at + 2, heads))) for at in range(0, heads, 2)]
    cuts = [slice(each[0] * HD, (each[-1] + 1) * HD) for each in sets]

    def diagonal(each):
        bands = [
            jnp.concatenate(
                [chosen[:, head * HD : (head + 1) * HD] if other == head else zero for other in each],
                axis=1,
            )
            for head in each
        ]
        return jnp.concatenate(bands, axis=0).astype(bf16)

    scores = [
        lax.dot_general(
            diagonal(each), keys[:, cut], (((1,), (1,)), ((), ())), preferred_element_type=f32
        )
        for each, cut in zip(sets, cuts)
    ]
    tops = jnp.zeros((rows, LANES), f32)
    weights, denoms = [], []
    for each, score in zip(sets, scores):
        wide = jnp.concatenate([live] * len(each), axis=0)
        score = jnp.where(wide, score * (1.0 / math.sqrt(HD)), floor_score)
        top = jnp.max(score, axis=1, keepdims=True)
        weight = jnp.where(wide, jnp.exp(score - top), 0.0).astype(bf16)
        denom = jnp.sum(weight.astype(f32), axis=1, keepdims=True)
        denom = jnp.where(denom > 0.0, denom, 1.0)
        weights.append(weight)
        denoms.append(denom)
        for at, head in enumerate(each):
            part = slice(at * rows, (at + 1) * rows)
            tops = jnp.where(lane == head, top[part] + jnp.log(denom[part]), tops)
    found = []
    for each, cut, weight, denom in zip(sets, cuts, weights, denoms):
        numer = jnp.dot(weight, values[:, cut], preferred_element_type=f32) / denom
        for at in range(len(each)):
            found.append(numer[at * rows : (at + 1) * rows, at * HD : (at + 1) * HD])
    spread = functools.partial(
        lax.dot_general, dimension_numbers=(((0,), (0,)), ((), ())), preferred_element_type=f32
    )
    dense = spread(pick[...], jnp.concatenate(found, axis=1).astype(bf16)).astype(bf16)
    stat = jnp.where(lane == LANES - 1, 1.0, split_top(tops)).astype(bf16)
    stat = spread(pick[...], stat)
    place = lax.broadcasted_iota(jnp.int32, stat.shape, 1)
    absent = stat[:, LANES - 1 :] == 0.0
    stat = jnp.where(absent & (place < STAT), floor_score, stat).astype(bf16)
    for out, part in ((keep, slice(0, half)), (send, slice(half, 2 * half))):
        out[:, : heads * HD] = dense[part]
        out[:, heads * HD :] = stat[part]


def merge(parts, tops):
    best = functools.reduce(jnp.maximum, tops)
    weights = [jnp.exp(top - best) for top in tops]
    total = functools.reduce(jnp.add, weights)
    shares = [weight / total for weight in weights]

    def head_of(head):
        terms = [
            share[:, head : head + 1] * part(head) for share, part in zip(shares, parts)
        ]
        return functools.reduce(jnp.add, terms)

    return head_of, best + jnp.log(total)


def part_of(ref):
    return lambda head: ref[:, head * HD : (head + 1) * HD].astype(f32)


def top_of(ref):
    return join_top(ref[:, ref.shape[1] - LANES :].astype(f32))


def merge_kernel(count, *refs):
    ins, outs = refs[:count], refs[count:]
    heads = ins[0].shape[1] // HD - 1
    rows = outs[0].shape[0]
    head_of, top = merge([part_of(ref) for ref in ins], [top_of(ref) for ref in ins])
    for head in range(heads + 1):
        cut = slice(head * HD, (head + 1) * HD)
        block = head_of(head) if head < heads else split_top(top)
        for at, out in enumerate(outs):
            out[:, cut] = block[at * rows : (at + 1) * rows].astype(bf16)


def last_kernel(count, *refs):
    ins = refs[:count]
    new_values, own_top, out = refs[count:]
    head_of, _ = merge(
        [part_of(ref) for ref in ins] + [part_of(new_values)],
        [top_of(ref) for ref in ins] + [own_top[...]],
    )
    for head in range(out.shape[1] // HD):
        out[:, head * HD : (head + 1) * HD] = head_of(head).astype(bf16)


def project_kernel(mid, own_rows, count, *refs):
    blocks, weight, outs, acc = refs[:count], refs[count], refs[count + 1 : -1], refs[-1]
    acc[...] = lax.dot_general(
        stacked(blocks).astype(bf16),
        weight[...],
        (((1,), (1,)), ((), ())),
        preferred_element_type=f32,
    )
    here = lax.axis_index("kv")
    owners = outs[0].shape[0] // own_rows
    for distance, out in enumerate(outs):
        side = lax.bitwise_xor(lax.axis_index("tp"), distance)
        rows = []
        for at in range(owners):
            offset = lax.bitwise_xor(side * owners + at, here)
            start = pl.multiple_of(place_of(offset, mid) * own_rows, own_rows)
            rows.append(acc[pl.ds(start, own_rows), :])
        out[...] = jnp.concatenate(rows, axis=0).astype(out.dtype)


def base_kernel(kept, residual, bias, total):
    total[...] = kept[...] + residual[...].astype(f32) + bias[...].astype(f32)


def final_kernel(total, *refs):
    value = total[...]
    for part in refs[:-1]:
        value = value + part[...].astype(f32)
    refs[-1][...] = value.astype(bf16)


def hop(x, axis, count, distance):
    return lax.ppermute(x, axis, [(i, i ^ distance) for i in range(count)])


def on_device(
    kv_count,
    tp_count,
    queries,
    new_keys,
    new_values,
    keys,
    values,
    slot_request,
    slot_valid,
    out_weight,
    out_bias,
    residual,
):
    own_rows, width = queries.shape
    slots = keys.shape[0]
    mid = kv_count // (2 * OUTER)
    requests = kv_count * own_rows
    rows = -(-(slots // PAGE) // 16) * 16
    wide = width + LANES
    kv_hop = lambda x, distance: hop(x, "kv", kv_count, distance)
    shaped = jax.ShapeDtypeStruct

    def call(kernel, shapes, scratch, name, *operands, spec=lambda at: WHOLE):
        single = not isinstance(shapes, tuple)
        return pl.pallas_call(
            kernel,
            out_shape=shapes,
            in_specs=[spec(at) for at in range(len(operands))],
            out_specs=WHOLE if single else (WHOLE,) * len(shapes),
            scratch_shapes=scratch,
            compiler_params=params(),
            name=name,
        )(*operands)

    def pack(parts, after):
        return call(
            functools.partial(pack_kernel, len(parts)),
            shaped((sum(x.shape[0] for x in parts), width), bf16),
            [],
            "pack",
            *parts,
            *after,
            spec=lambda at: WHOLE if at < len(parts) else ANY,
        )

    def gather(block, last, before, after):
        near = pack([kv_hop(block, 2 * mid * far) for far in (3, 2, 1)] + [last], before)
        far = [kv_hop(near, 2 * middle) for middle in range(1, mid)]
        if after:
            far = [pack(far, after)]
        line = [near] + far
        return line + [kv_hop(x, 1) for x in line]

    pick, mask, own_top, held = call(
        functools.partial(prep_kernel, mid, own_rows),
        (
            shaped((rows, requests), bf16),
            shaped((rows, slots), f32),
            shaped((own_rows, LANES), f32),
            shaped(queries.shape, bf16),
        ),
        [],
        "prep",
        slot_request.reshape(1, slots),
        slot_valid.reshape(1, slots),
        queries,
        new_keys,
    )
    ready = call(ready_kernel, shaped((8, LANES), f32), [], "ready", keys, values, spec=lambda at: ANY)
    blocks = gather(queries, held, [pick], [ready])
    half = requests // 2
    keep, send = call(
        functools.partial(attend_kernel, len(blocks)),
        (shaped((half, wide), bf16),) * 2,
        [],
        "attend",
        pick,
        mask,
        keys,
        values,
        *blocks,
    )

    def merged(ins, count):
        size = ins[0].shape[0] // count
        return call(
            functools.partial(merge_kernel, len(ins)),
            (shaped((size, wide), bf16),) * count,
            [],
            "merge",
            *ins,
        )

    blocks = merged([keep, kv_hop(send, 1)], 2 * mid)
    outer = []
    for at in (0, 1):
        there = [kv_hop(blocks[2 * near + at], 2 * near) for near in range(1, mid)]
        outer += merged([blocks[at]] + there, 2)
    ins = [outer[3]] + [kv_hop(outer[OUTER - 1 - far], 2 * mid * far) for far in (3, 2, 1)]
    attended = call(
        functools.partial(last_kernel, len(ins)),
        shaped((own_rows, width), bf16),
        [],
        "last",
        *ins,
        new_values,
        own_top,
    )

    blocks = gather(attended, attended, [], [])
    columns = out_weight.shape[1]
    shape = (requests // tp_count, columns)
    kept, *sent = call(
        functools.partial(project_kernel, mid, own_rows, len(blocks)),
        (shaped(shape, f32),) + (shaped(shape, SENT),) * (tp_count - 1),
        [pltpu.VMEM((requests, columns), f32)],
        "project",
        *blocks,
        out_weight.T,
    )
    received = [hop(x, "tp", tp_count, at + 1) for at, x in enumerate(sent)]
    total = call(
        base_kernel, shaped(shape, f32), [], "base", kept, residual, out_bias.reshape(1, columns)
    )
    return call(final_kernel, shaped(shape, bf16), [], "final", total, *received)


def solution(mesh):
    placed = (
        P("kv", "tp"),
        P("kv", "tp"),
        P("kv", "tp"),
        P("kv", "tp"),
        P("kv", "tp"),
        P("kv"),
        P("kv"),
        P("tp", "kv"),
        P("kv"),
        P("tp", "kv"),
    )
    return jax.shard_map(
        functools.partial(on_device, mesh.shape["kv"], mesh.shape["tp"]),
        mesh=mesh,
        in_specs=placed,
        out_specs=P("tp", "kv"),
        check_vma=False,
    )
```

```python
import functools
import math

import jax
import jax.numpy as jnp
from jax import lax
from jax.experimental import pallas as pl
from jax.experimental.pallas import tpu as pltpu
from jax.sharding import PartitionSpec as P

HD = 128
PAGE = 16
OUTER = 4
LANES = 128
STAT = 32

floor_score = -1e30
SENT = jnp.bfloat16
GATHER_DIRECT = 1
REDUCE_DIRECT = 3
f32 = jnp.float32
bf16 = jnp.bfloat16
WHOLE = pl.BlockSpec(memory_space=pltpu.VMEM)
ANY = pl.BlockSpec(memory_space=pl.ANY)


def params(megabytes=24):
    return pltpu.CompilerParams(vmem_limit_bytes=megabytes * 1024 * 1024)


def relayed(direct):
    return [far for far in (3, 2, 1) if far != direct]


def gather_order(mid, direct):
    lines = [[(far, 0) for far in relayed(direct) + [0, direct]]]
    lines[0] += [(direct, middle) for middle in range(1, mid)]
    lines += [[(far, middle) for far in relayed(direct) + [0]] for middle in range(1, mid)]
    return [
        core + 2 * middle + 2 * mid * far
        for core in (0, 1)
        for line in lines
        for far, middle in line
    ]


def reduce_order(mid, direct):
    return [
        core + 2 * middle + 2 * mid * far
        for core in (0, 1)
        for middle in range(mid)
        for far in relayed(direct) + [0, direct]
    ]


def request_at(place, order, own_rows):
    distance = jnp.zeros_like(place)
    for at, value in enumerate(order):
        distance = jnp.where(place // own_rows == at, value, distance)
    return lax.bitwise_xor(distance, lax.axis_index("kv")) * own_rows + place % own_rows


def prep_kernel(mid, own_rows, request, valid, pick, spread, mask):
    rows, slots = mask.shape
    row = lax.broadcasted_iota(jnp.int32, (rows, slots), 0)
    lane = lax.broadcasted_iota(jnp.int32, (rows, slots), 1)
    owners = jnp.broadcast_to(request[...], (rows, slots))
    mine = jnp.sum(jnp.where(lane == row * PAGE, owners, 0), axis=1, keepdims=True)
    before = jnp.sum(jnp.where(lane == row * PAGE - PAGE, owners, 0), axis=1, keepdims=True)
    page = lax.broadcasted_iota(jnp.int32, (rows, 1), 0)
    first = ((page == 0) | (mine != before)) & (page < slots // PAGE)
    live = (owners == mine) & first & (jnp.broadcast_to(valid[...], (rows, slots)) == 1)
    mask[...] = jnp.where(live, 1.0, 0.0)
    place = lax.broadcasted_iota(jnp.int32, pick.shape, 1)
    orders = (gather_order(mid, GATHER_DIRECT), reduce_order(mid, REDUCE_DIRECT))
    for out, order in zip((pick, spread), orders):
        named = request_at(place, order, own_rows)
        out[...] = jnp.where((named == mine) & first, 1.0, 0.0).astype(bf16)


def own_kernel(queries, new_keys, own_top):
    where = lax.broadcasted_iota(jnp.int32, own_top.shape, 1)
    top = jnp.zeros(own_top.shape, f32)
    for head in range(queries.shape[1] // HD):
        cut = slice(head * HD, (head + 1) * HD)
        score = jnp.sum(
            queries[:, cut].astype(f32) * new_keys[:, cut].astype(f32), axis=1, keepdims=True
        ) * (1.0 / math.sqrt(HD))
        top = jnp.where(where == head, score, top)
    own_top[...] = top


def split_top(top):
    lane = lax.broadcasted_iota(jnp.int32, top.shape, 1)
    top = jnp.where(lane < STAT, top, 0.0)
    high = top.astype(bf16).astype(f32)
    rest = top - high
    middle = rest.astype(bf16).astype(f32)
    low = rest - middle
    return high + pltpu.roll(middle, STAT, 1) + pltpu.roll(low, 2 * STAT, 1)


def join_top(stat):
    return (stat + pltpu.roll(stat, LANES - STAT, 1)) + pltpu.roll(stat, LANES - 2 * STAT, 1)


def stacked(refs):
    return jnp.concatenate([ref[...].astype(f32) for ref in refs], axis=0)


def pack_kernel(count, *refs):
    refs[-1][...] = stacked(refs[:count]).astype(bf16)


def hold_kernel(queries, held):
    held[...] = queries[...]


def ready_kernel(*refs):
    refs[-1][...] = jnp.zeros_like(refs[-1])


def attend_kernel(count, pick, spread_to, mask, keys, values, *refs):
    blocks, outs = refs[:count], refs[count:]
    rows = pick.shape[0]
    heads = keys.shape[1] // HD
    lane = lax.broadcasted_iota(jnp.int32, (rows, LANES), 1)
    live = mask[...] > 0.0
    chosen = jnp.dot(pick[...], stacked(blocks).astype(bf16), preferred_element_type=f32)
    zero = jnp.zeros((rows, HD), f32)
    sets = [tuple(range(at, min(at + 2, heads))) for at in range(0, heads, 2)]
    cuts = [slice(each[0] * HD, (each[-1] + 1) * HD) for each in sets]

    def diagonal(each):
        bands = [
            jnp.concatenate(
                [chosen[:, head * HD : (head + 1) * HD] if other == head else zero for other in each],
                axis=1,
            )
            for head in each
        ]
        return jnp.concatenate(bands, axis=0).astype(bf16)

    scores = [
        lax.dot_general(
            diagonal(each), keys[:, cut], (((1,), (1,)), ((), ())), preferred_element_type=f32
        )
        for each, cut in zip(sets, cuts)
    ]
    tops = jnp.zeros((rows, LANES), f32)
    weights, denoms = [], []
    for each, score in zip(sets, scores):
        wide = jnp.concatenate([live] * len(each), axis=0)
        score = jnp.where(wide, score * (1.0 / math.sqrt(HD)), floor_score)
        top = jnp.max(score, axis=1, keepdims=True)
        weight = jnp.where(wide, jnp.exp(score - top), 0.0).astype(bf16)
        denom = jnp.sum(weight.astype(f32), axis=1, keepdims=True)
        denom = jnp.where(denom > 0.0, denom, 1.0)
        weights.append(weight)
        denoms.append(denom)
        for at, head in enumerate(each):
            part = slice(at * rows, (at + 1) * rows)
            tops = jnp.where(lane == head, top[part] + jnp.log(denom[part]), tops)
    found = []
    for each, cut, weight, denom in zip(sets, cuts, weights, denoms):
        numer = jnp.dot(weight, values[:, cut], preferred_element_type=f32) / denom
        for at in range(len(each)):
            found.append(numer[at * rows : (at + 1) * rows, at * HD : (at + 1) * HD])
    spread = functools.partial(
        lax.dot_general, dimension_numbers=(((0,), (0,)), ((), ())), preferred_element_type=f32
    )
    dense = spread(spread_to[...], jnp.concatenate(found, axis=1).astype(bf16)).astype(bf16)
    stat = jnp.where(lane == LANES - 1, 1.0, split_top(tops)).astype(bf16)
    stat = spread(spread_to[...], stat)
    place = lax.broadcasted_iota(jnp.int32, stat.shape, 1)
    absent = stat[:, LANES - 1 :] == 0.0
    stat = jnp.where(absent & (place < STAT), floor_score, stat).astype(bf16)
    size = outs[0].shape[0]
    for at, out in enumerate(outs):
        part = slice(at * size, (at + 1) * size)
        out[:, : heads * HD] = dense[part]
        out[:, heads * HD :] = stat[part]


def merge(parts, tops):
    best = functools.reduce(jnp.maximum, tops)
    weights = [jnp.exp(top - best) for top in tops]
    total = functools.reduce(jnp.add, weights)
    shares = [weight / total for weight in weights]

    def head_of(head):
        terms = [
            share[:, head : head + 1] * part(head) for share, part in zip(shares, parts)
        ]
        return functools.reduce(jnp.add, terms)

    return head_of, best + jnp.log(total)


def part_of(ref, start, rows):
    return lambda head: ref[:, head * HD : (head + 1) * HD].astype(f32)[start : start + rows]


def top_of(ref, start, rows):
    return join_top(ref[:, ref.shape[1] - LANES :].astype(f32)[start : start + rows])


def merge_kernel(count, *refs):
    ins, outs = refs[:count], refs[count:]
    heads = ins[0].shape[1] // HD - 1
    rows = sum(out.shape[0] for out in outs)
    head_of, top = merge(
        [part_of(ref, 0, rows) for ref in ins], [top_of(ref, 0, rows) for ref in ins]
    )
    for head in range(heads + 1):
        cut = slice(head * HD, (head + 1) * HD)
        block = head_of(head) if head < heads else split_top(top)
        at = 0
        for out in outs:
            out[:, cut] = block[at : at + out.shape[0]].astype(bf16)
            at += out.shape[0]


def last_kernel(count, *refs):
    ins = refs[:count]
    new_values, own_top, out = refs[count:]
    rows = out.shape[0]
    head_of, _ = merge(
        [part_of(ref, ref.shape[0] - rows, rows) for ref in ins] + [part_of(new_values, 0, rows)],
        [top_of(ref, ref.shape[0] - rows, rows) for ref in ins] + [own_top[...]],
    )
    for head in range(out.shape[1] // HD):
        out[:, head * HD : (head + 1) * HD] = head_of(head).astype(bf16)


def project_kernel(mid, own_rows, count, *refs):
    blocks, weight, outs, acc = refs[:count], refs[count], refs[count + 1 : -1], refs[-1]
    product = lax.dot_general(
        stacked(blocks).astype(bf16),
        weight[...],
        (((1,), (1,)), ((), ())),
        preferred_element_type=f32,
    )
    for at, distance in enumerate(gather_order(mid, GATHER_DIRECT)):
        owner = lax.bitwise_xor(lax.axis_index("kv"), distance)
        start = pl.multiple_of(owner * own_rows, own_rows)
        acc[pl.ds(start, own_rows), :] = product[at * own_rows : (at + 1) * own_rows]
    for distance, out in enumerate(outs):
        rows = out.shape[0]
        side = lax.bitwise_xor(lax.axis_index("tp"), distance)
        out[...] = acc[pl.ds(pl.multiple_of(side * rows, rows), rows), :].astype(out.dtype)


def base_kernel(kept, residual, bias, total):
    total[...] = kept[...] + residual[...].astype(f32) + bias[...].astype(f32)


def final_kernel(total, *refs):
    value = total[...]
    for part in refs[:-1]:
        value = value + part[...].astype(f32)
    refs[-1][...] = value.astype(bf16)


def hop(x, axis, count, distance):
    return lax.ppermute(x, axis, [(i, i ^ distance) for i in range(count)])


def on_device(
    kv_count,
    tp_count,
    queries,
    new_keys,
    new_values,
    keys,
    values,
    slot_request,
    slot_valid,
    out_weight,
    out_bias,
    residual,
):
    own_rows, width = queries.shape
    slots = keys.shape[0]
    mid = kv_count // (2 * OUTER)
    requests = kv_count * own_rows
    rows = -(-(slots // PAGE) // 16) * 16
    wide = width + LANES
    kv_hop = lambda x, distance: hop(x, "kv", kv_count, distance)
    shaped = jax.ShapeDtypeStruct

    def call(kernel, shapes, scratch, name, *operands, spec=lambda at: WHOLE):
        single = not isinstance(shapes, tuple)
        return pl.pallas_call(
            kernel,
            out_shape=shapes,
            in_specs=[spec(at) for at in range(len(operands))],
            out_specs=WHOLE if single else (WHOLE,) * len(shapes),
            scratch_shapes=scratch,
            compiler_params=params(),
            name=name,
        )(*operands)

    def pack(parts, *after):
        return call(
            functools.partial(pack_kernel, len(parts)),
            shaped((sum(x.shape[0] for x in parts), width), bf16),
            [],
            "pack",
            *parts,
            *after,
            spec=lambda at: WHOLE if at < len(parts) else ANY,
        )

    def gather(block, own, before, after):
        outer = {far: kv_hop(block, 2 * mid * far) for far in (3, 2, 1)}
        across = [
            kv_hop(block, 2 * middle + 2 * mid * GATHER_DIRECT) for middle in range(1, mid)
        ]
        relay = pack([outer[far] for far in relayed(GATHER_DIRECT)] + [own], *before)
        near = pack([relay, outer[GATHER_DIRECT], *across])
        far = [kv_hop(relay, 2 * middle) for middle in range(1, mid)]
        if after:
            far = [pack(far, *after)]
        line = [near] + far
        return line + [kv_hop(x, 1) for x in line]

    pick, spread_to, mask = call(
        functools.partial(prep_kernel, mid, own_rows),
        (
            shaped((rows, requests), bf16),
            shaped((rows, requests), bf16),
            shaped((rows, slots), f32),
        ),
        [],
        "prep",
        slot_request.reshape(1, slots),
        slot_valid.reshape(1, slots),
    )
    held = call(hold_kernel, shaped(queries.shape, bf16), [], "hold", queries)
    own_top = call(own_kernel, shaped((own_rows, LANES), f32), [], "own", held, new_keys)
    ready = [
        call(ready_kernel, shaped((8, LANES), f32), [], "ready", x, spec=lambda at: ANY)
        for x in (keys, values)
    ]
    blocks = gather(queries, held, [ready[0]], [ready[1], pick, own_top])
    size = OUTER * own_rows
    outs = call(
        functools.partial(attend_kernel, len(blocks)),
        (shaped((size, wide), bf16),) * (2 * mid),
        [],
        "attend",
        pick,
        spread_to,
        mask,
        keys,
        values,
        *blocks,
    )

    def merged(ins, *heights):
        return call(
            functools.partial(merge_kernel, len(ins)),
            tuple(shaped((height * own_rows, wide), bf16) for height in heights),
            [],
            "merge",
            *ins,
        )

    relays, ins = [], []
    for middle in range(1, mid):
        relay, straight = merged([outs[middle], kv_hop(outs[mid + middle], 1)], 3, 1)
        relays.append(kv_hop(relay, 2 * middle))
        ins.append(kv_hop(straight, 2 * middle + 2 * mid * REDUCE_DIRECT))
    *pair, own, straight = merged([outs[0], kv_hop(outs[mid], 1)], 2, 1, 1)
    pair = merged(pair + relays, 1, 1)
    ins += [own, *relays, kv_hop(straight, 2 * mid * REDUCE_DIRECT)]
    ins += [kv_hop(x, 2 * mid * far) for x, far in zip(pair, relayed(REDUCE_DIRECT))]
    attended = call(
        functools.partial(last_kernel, len(ins)),
        shaped((own_rows, width), bf16),
        [],
        "last",
        *ins,
        new_values,
        own_top,
    )

    blocks = gather(attended, attended, [], [])
    columns = out_weight.shape[1]
    shape = (requests // tp_count, columns)
    kept, *sent = call(
        functools.partial(project_kernel, mid, own_rows, len(blocks)),
        (shaped(shape, f32),) + (shaped(shape, SENT),) * (tp_count - 1),
        [pltpu.VMEM((requests, columns), f32)],
        "project",
        *blocks,
        out_weight.T,
    )
    received = [hop(x, "tp", tp_count, at + 1) for at, x in enumerate(sent)]
    total = call(
        base_kernel, shaped(shape, f32), [], "base", kept, residual, out_bias.reshape(1, columns)
    )
    return call(final_kernel, shaped(shape, bf16), [], "final", total, *received)


def solution(mesh):
    placed = (
        P("kv", "tp"),
        P("kv", "tp"),
        P("kv", "tp"),
        P("kv", "tp"),
        P("kv", "tp"),
        P("kv"),
        P("kv"),
        P("tp", "kv"),
        P("kv"),
        P("tp", "kv"),
    )
    return jax.shard_map(
        functools.partial(on_device, mesh.shape["kv"], mesh.shape["tp"]),
        mesh=mesh,
        in_specs=placed,
        out_specs=P("tp", "kv"),
        check_vma=False,
    )
```

```python
import functools
import math

import jax
import jax.numpy as jnp
from jax import lax
from jax.experimental import pallas as pl
from jax.experimental.pallas import tpu as pltpu
from jax.sharding import PartitionSpec as P

HD = 128
PAGE = 16
OUTER = 4
LANES = 128
STAT = 32

floor_score = -1e30
SENT = jnp.bfloat16
QUERY_ORDER = (3, 2, 1)
REDUCE_ORDER = (2, 1, 3)
RESULT_ORDER = (3, 2, 1)
f32 = jnp.float32
bf16 = jnp.bfloat16
WHOLE = pl.BlockSpec(memory_space=pltpu.VMEM)
ANY = pl.BlockSpec(memory_space=pl.ANY)


def params(megabytes=24):
    return pltpu.CompilerParams(vmem_limit_bytes=megabytes * 1024 * 1024)


def relayed(order):
    return list(order[:2])


def gather_order(mid, order):
    lines = [[(far, 0) for far in relayed(order) + [0, order[2]]]]
    lines[0] += [(order[2], middle) for middle in range(1, mid)]
    lines += [[(far, middle) for far in relayed(order) + [0]] for middle in range(1, mid)]
    return [
        core + 2 * middle + 2 * mid * far
        for core in (0, 1)
        for line in lines
        for far, middle in line
    ]


def reduce_order(mid, order):
    return [
        core + 2 * middle + 2 * mid * far
        for core in (0, 1)
        for middle in range(mid)
        for far in relayed(order) + [0, order[2]]
    ]


def request_at(place, order, own_rows):
    distance = jnp.zeros_like(place)
    for at, value in enumerate(order):
        distance = jnp.where(place // own_rows == at, value, distance)
    return lax.bitwise_xor(distance, lax.axis_index("kv")) * own_rows + place % own_rows


def prep_kernel(mid, own_rows, request, valid, pick, spread, mask):
    rows, slots = mask.shape
    row = lax.broadcasted_iota(jnp.int32, (rows, slots), 0)
    lane = lax.broadcasted_iota(jnp.int32, (rows, slots), 1)
    owners = jnp.broadcast_to(request[...], (rows, slots))
    mine = jnp.sum(jnp.where(lane == row * PAGE, owners, 0), axis=1, keepdims=True)
    before = jnp.sum(jnp.where(lane == row * PAGE - PAGE, owners, 0), axis=1, keepdims=True)
    page = lax.broadcasted_iota(jnp.int32, (rows, 1), 0)
    first = ((page == 0) | (mine != before)) & (page < slots // PAGE)
    live = (owners == mine) & first & (jnp.broadcast_to(valid[...], (rows, slots)) == 1)
    mask[...] = jnp.where(live, 1.0, 0.0)
    place = lax.broadcasted_iota(jnp.int32, pick.shape, 1)
    orders = (gather_order(mid, QUERY_ORDER), reduce_order(mid, REDUCE_ORDER))
    for out, order in zip((pick, spread), orders):
        named = request_at(place, order, own_rows)
        out[...] = jnp.where((named == mine) & first, 1.0, 0.0).astype(bf16)


def own_kernel(queries, new_keys, own_top):
    where = lax.broadcasted_iota(jnp.int32, own_top.shape, 1)
    top = jnp.zeros(own_top.shape, f32)
    for head in range(queries.shape[1] // HD):
        cut = slice(head * HD, (head + 1) * HD)
        score = jnp.sum(
            queries[:, cut].astype(f32) * new_keys[:, cut].astype(f32), axis=1, keepdims=True
        ) * (1.0 / math.sqrt(HD))
        top = jnp.where(where == head, score, top)
    own_top[...] = top


def split_top(top):
    lane = lax.broadcasted_iota(jnp.int32, top.shape, 1)
    top = jnp.where(lane < STAT, top, 0.0)
    high = top.astype(bf16).astype(f32)
    rest = top - high
    middle = rest.astype(bf16).astype(f32)
    low = rest - middle
    return high + pltpu.roll(middle, STAT, 1) + pltpu.roll(low, 2 * STAT, 1)


def join_top(stat):
    return (stat + pltpu.roll(stat, LANES - STAT, 1)) + pltpu.roll(stat, LANES - 2 * STAT, 1)


def stacked(refs):
    return jnp.concatenate([ref[...].astype(f32) for ref in refs], axis=0)


def pack_kernel(count, *refs):
    refs[-1][...] = stacked(refs[:count]).astype(bf16)


def hold_kernel(queries, held):
    held[...] = queries[...]


def ready_kernel(*refs):
    refs[-1][...] = jnp.zeros_like(refs[-1])


def attend_kernel(count, pick, spread_to, mask, keys, values, *refs):
    blocks, outs = refs[:count], refs[count:]
    rows = pick.shape[0]
    heads = keys.shape[1] // HD
    lane = lax.broadcasted_iota(jnp.int32, (rows, LANES), 1)
    live = mask[...] > 0.0
    chosen = jnp.dot(pick[...], stacked(blocks).astype(bf16), preferred_element_type=f32)
    zero = jnp.zeros((rows, HD), f32)
    sets = [tuple(range(at, min(at + 2, heads))) for at in range(0, heads, 2)]
    cuts = [slice(each[0] * HD, (each[-1] + 1) * HD) for each in sets]

    def diagonal(each):
        bands = [
            jnp.concatenate(
                [chosen[:, head * HD : (head + 1) * HD] if other == head else zero for other in each],
                axis=1,
            )
            for head in each
        ]
        return jnp.concatenate(bands, axis=0).astype(bf16)

    scores = [
        lax.dot_general(
            diagonal(each), keys[:, cut], (((1,), (1,)), ((), ())), preferred_element_type=f32
        )
        for each, cut in zip(sets, cuts)
    ]
    tops = jnp.zeros((rows, LANES), f32)
    weights, denoms = [], []
    for each, score in zip(sets, scores):
        wide = jnp.concatenate([live] * len(each), axis=0)
        score = jnp.where(wide, score * (1.0 / math.sqrt(HD)), floor_score)
        top = jnp.max(score, axis=1, keepdims=True)
        weight = jnp.where(wide, jnp.exp(score - top), 0.0).astype(bf16)
        denom = jnp.sum(weight.astype(f32), axis=1, keepdims=True)
        denom = jnp.where(denom > 0.0, denom, 1.0)
        weights.append(weight)
        denoms.append(denom)
        for at, head in enumerate(each):
            part = slice(at * rows, (at + 1) * rows)
            tops = jnp.where(lane == head, top[part] + jnp.log(denom[part]), tops)
    found = []
    for each, cut, weight, denom in zip(sets, cuts, weights, denoms):
        numer = jnp.dot(weight, values[:, cut], preferred_element_type=f32) / denom
        for at in range(len(each)):
            found.append(numer[at * rows : (at + 1) * rows, at * HD : (at + 1) * HD])
    spread = functools.partial(
        lax.dot_general, dimension_numbers=(((0,), (0,)), ((), ())), preferred_element_type=f32
    )
    dense = spread(spread_to[...], jnp.concatenate(found, axis=1).astype(bf16)).astype(bf16)
    stat = jnp.where(lane == LANES - 1, 1.0, split_top(tops)).astype(bf16)
    stat = spread(spread_to[...], stat)
    place = lax.broadcasted_iota(jnp.int32, stat.shape, 1)
    absent = stat[:, LANES - 1 :] == 0.0
    stat = jnp.where(absent & (place < STAT), floor_score, stat).astype(bf16)
    size = outs[0].shape[0]
    for at, out in enumerate(outs):
        part = slice(at * size, (at + 1) * size)
        out[:, : heads * HD] = dense[part]
        out[:, heads * HD :] = stat[part]


def merge(parts, tops):
    best = functools.reduce(jnp.maximum, tops)
    weights = [jnp.exp(top - best) for top in tops]
    total = functools.reduce(jnp.add, weights)
    shares = [weight / total for weight in weights]

    def head_of(head):
        terms = [
            share[:, head : head + 1] * part(head) for share, part in zip(shares, parts)
        ]
        return functools.reduce(jnp.add, terms)

    return head_of, best + jnp.log(total)


def part_of(ref, start, rows):
    return lambda head: ref[:, head * HD : (head + 1) * HD].astype(f32)[start : start + rows]


def top_of(ref, start, rows):
    return join_top(ref[:, ref.shape[1] - LANES :].astype(f32)[start : start + rows])


def merge_kernel(count, *refs):
    ins, outs = refs[:count], refs[count:]
    heads = ins[0].shape[1] // HD - 1
    rows = sum(out.shape[0] for out in outs)
    head_of, top = merge(
        [part_of(ref, 0, rows) for ref in ins], [top_of(ref, 0, rows) for ref in ins]
    )
    for head in range(heads + 1):
        cut = slice(head * HD, (head + 1) * HD)
        block = head_of(head) if head < heads else split_top(top)
        at = 0
        for out in outs:
            out[:, cut] = block[at : at + out.shape[0]].astype(bf16)
            at += out.shape[0]


def last_kernel(count, *refs):
    ins = refs[:count]
    new_values, own_top, out = refs[count:]
    rows = out.shape[0]
    head_of, _ = merge(
        [part_of(ref, ref.shape[0] - rows, rows) for ref in ins] + [part_of(new_values, 0, rows)],
        [top_of(ref, ref.shape[0] - rows, rows) for ref in ins] + [own_top[...]],
    )
    for head in range(out.shape[1] // HD):
        out[:, head * HD : (head + 1) * HD] = head_of(head).astype(bf16)


def project_kernel(mid, own_rows, count, *refs):
    blocks, weight, outs, acc = refs[:count], refs[count], refs[count + 1 : -1], refs[-1]
    product = lax.dot_general(
        stacked(blocks).astype(bf16),
        weight[...],
        (((1,), (1,)), ((), ())),
        preferred_element_type=f32,
    )
    for at, distance in enumerate(gather_order(mid, RESULT_ORDER)):
        owner = lax.bitwise_xor(lax.axis_index("kv"), distance)
        start = pl.multiple_of(owner * own_rows, own_rows)
        acc[pl.ds(start, own_rows), :] = product[at * own_rows : (at + 1) * own_rows]
    for distance, out in enumerate(outs):
        rows = out.shape[0]
        side = lax.bitwise_xor(lax.axis_index("tp"), distance)
        out[...] = acc[pl.ds(pl.multiple_of(side * rows, rows), rows), :].astype(out.dtype)


def base_kernel(kept, residual, bias, total):
    total[...] = kept[...] + residual[...].astype(f32) + bias[...].astype(f32)


def final_kernel(total, *refs):
    value = total[...]
    for part in refs[:-1]:
        value = value + part[...].astype(f32)
    refs[-1][...] = value.astype(bf16)


def hop(x, axis, count, distance):
    return lax.ppermute(x, axis, [(i, i ^ distance) for i in range(count)])


def on_device(
    kv_count,
    tp_count,
    queries,
    new_keys,
    new_values,
    keys,
    values,
    slot_request,
    slot_valid,
    out_weight,
    out_bias,
    residual,
):
    own_rows, width = queries.shape
    slots = keys.shape[0]
    mid = kv_count // (2 * OUTER)
    requests = kv_count * own_rows
    rows = -(-(slots // PAGE) // 16) * 16
    wide = width + LANES
    kv_hop = lambda x, distance: hop(x, "kv", kv_count, distance)
    shaped = jax.ShapeDtypeStruct

    def call(kernel, shapes, scratch, name, *operands, spec=lambda at: WHOLE):
        single = not isinstance(shapes, tuple)
        return pl.pallas_call(
            kernel,
            out_shape=shapes,
            in_specs=[spec(at) for at in range(len(operands))],
            out_specs=WHOLE if single else (WHOLE,) * len(shapes),
            scratch_shapes=scratch,
            compiler_params=params(),
            name=name,
        )(*operands)

    def pack(parts, *after):
        return call(
            functools.partial(pack_kernel, len(parts)),
            shaped((sum(x.shape[0] for x in parts), width), bf16),
            [],
            "pack",
            *parts,
            *after,
            spec=lambda at: WHOLE if at < len(parts) else ANY,
        )

    def gather(block, own, order, before, after, beside):
        outer = {far: kv_hop(block, 2 * mid * far) for far in order}
        across = [
            kv_hop(block, 2 * middle + 2 * mid * order[2]) for middle in range(1, mid)
        ]
        relay = pack([outer[far] for far in relayed(order)] + [own], *before)
        near = pack([relay, outer[order[2]], *across], *beside)
        far = [kv_hop(relay, 2 * middle) for middle in range(1, mid)]
        if after:
            far = [pack(far, *after)]
        line = [near] + far
        return line + [kv_hop(x, 1) for x in line]

    pick, spread_to, mask = call(
        functools.partial(prep_kernel, mid, own_rows),
        (
            shaped((rows, requests), bf16),
            shaped((rows, requests), bf16),
            shaped((rows, slots), f32),
        ),
        [],
        "prep",
        slot_request.reshape(1, slots),
        slot_valid.reshape(1, slots),
    )
    held = call(hold_kernel, shaped(queries.shape, bf16), [], "hold", queries)
    own_top = call(own_kernel, shaped((own_rows, LANES), f32), [], "own", held, new_keys)
    ready = [
        call(ready_kernel, shaped((8, LANES), f32), [], "ready", x, spec=lambda at: ANY)
        for x in (keys, values)
    ]
    blocks = gather(queries, held, QUERY_ORDER, [own_top], [ready[0], pick], [ready[1]])
    size = OUTER * own_rows
    outs = call(
        functools.partial(attend_kernel, len(blocks)),
        (shaped((size, wide), bf16),) * (2 * mid),
        [],
        "attend",
        pick,
        spread_to,
        mask,
        keys,
        values,
        *blocks,
    )

    def merged(ins, *heights):
        return call(
            functools.partial(merge_kernel, len(ins)),
            tuple(shaped((height * own_rows, wide), bf16) for height in heights),
            [],
            "merge",
            *ins,
        )

    relays, ins = [], []
    for middle in range(1, mid):
        relay, straight = merged([outs[middle], kv_hop(outs[mid + middle], 1)], 3, 1)
        relays.append(kv_hop(relay, 2 * middle))
        ins.append(kv_hop(straight, 2 * middle + 2 * mid * REDUCE_ORDER[2]))
    *pair, own, straight = merged([outs[0], kv_hop(outs[mid], 1)], 2, 1, 1)
    pair = merged(pair + relays, 1, 1)
    ins += [own, *relays, kv_hop(straight, 2 * mid * REDUCE_ORDER[2])]
    ins += [kv_hop(x, 2 * mid * far) for x, far in zip(pair, relayed(REDUCE_ORDER))]
    attended = call(
        functools.partial(last_kernel, len(ins)),
        shaped((own_rows, width), bf16),
        [],
        "last",
        *ins,
        new_values,
        own_top,
    )

    blocks = gather(attended, attended, RESULT_ORDER, [], [], [])
    columns = out_weight.shape[1]
    shape = (requests // tp_count, columns)
    kept, *sent = call(
        functools.partial(project_kernel, mid, own_rows, len(blocks)),
        (shaped(shape, f32),) + (shaped(shape, SENT),) * (tp_count - 1),
        [pltpu.VMEM((requests, columns), f32)],
        "project",
        *blocks,
        out_weight.T,
    )
    received = [hop(x, "tp", tp_count, at + 1) for at, x in enumerate(sent)]
    total = call(
        base_kernel, shaped(shape, f32), [], "base", kept, residual, out_bias.reshape(1, columns)
    )
    return call(final_kernel, shaped(shape, bf16), [], "final", total, *received)


def solution(mesh):
    placed = (
        P("kv", "tp"),
        P("kv", "tp"),
        P("kv", "tp"),
        P("kv", "tp"),
        P("kv", "tp"),
        P("kv"),
        P("kv"),
        P("tp", "kv"),
        P("kv"),
        P("tp", "kv"),
    )
    return jax.shard_map(
        functools.partial(on_device, mesh.shape["kv"], mesh.shape["tp"]),
        mesh=mesh,
        in_specs=placed,
        out_specs=P("tp", "kv"),
        check_vma=False,
    )
```

```python
import functools
import math

import jax
import jax.numpy as jnp
from jax import lax
from jax.experimental import pallas as pl
from jax.experimental.pallas import tpu as pltpu
from jax.sharding import PartitionSpec as P

HD = 128
PAGE = 16
OUTER = 4
LANES = 128
LAG = 3
STAT = 32

floor_score = -1e30
SENT = jnp.bfloat16
QUERY_ORDER = (3, 2, 1)
REDUCE_ORDER = (2, 1, 3)
RESULT_ORDER = (3, 2, 1)
f32 = jnp.float32
bf16 = jnp.bfloat16
WHOLE = pl.BlockSpec(memory_space=pltpu.VMEM)
ANY = pl.BlockSpec(memory_space=pl.ANY)


def params(megabytes=24):
    return pltpu.CompilerParams(vmem_limit_bytes=megabytes * 1024 * 1024)


def relayed(order):
    return list(order[:2])


def gather_order(mid, order):
    lines = [[(far, 0) for far in relayed(order) + [0, order[2]]]]
    lines[0] += [(order[2], middle) for middle in range(1, mid)]
    lines += [[(far, middle) for far in relayed(order) + [0]] for middle in range(1, mid)]
    return [
        core + 2 * middle + 2 * mid * far
        for core in (0, 1)
        for line in lines
        for far, middle in line
    ]


def reduce_order(mid, order):
    return [
        core + 2 * middle + 2 * mid * far
        for core in (0, 1)
        for middle in range(mid)
        for far in relayed(order) + [0, order[2]]
    ]


def request_at(place, order, own_rows):
    distance = jnp.zeros_like(place)
    for at, value in enumerate(order):
        distance = jnp.where(place // own_rows == at, value, distance)
    return lax.bitwise_xor(distance, lax.axis_index("kv")) * own_rows + place % own_rows


def prep_kernel(mid, own_rows, request, valid, pick, spread, mask):
    rows, slots = mask.shape
    row = lax.broadcasted_iota(jnp.int32, (rows, slots), 0)
    lane = lax.broadcasted_iota(jnp.int32, (rows, slots), 1)
    owners = jnp.broadcast_to(request[...], (rows, slots))
    mine = jnp.sum(jnp.where(lane == row * PAGE, owners, 0), axis=1, keepdims=True)
    before = jnp.sum(jnp.where(lane == row * PAGE - PAGE, owners, 0), axis=1, keepdims=True)
    page = lax.broadcasted_iota(jnp.int32, (rows, 1), 0)
    first = ((page == 0) | (mine != before)) & (page < slots // PAGE)
    live = (owners == mine) & first & (jnp.broadcast_to(valid[...], (rows, slots)) == 1)
    mask[...] = jnp.where(live, 1.0, 0.0)
    place = lax.broadcasted_iota(jnp.int32, pick.shape, 1)
    orders = (gather_order(mid, QUERY_ORDER), reduce_order(mid, REDUCE_ORDER))
    for out, order in zip((pick, spread), orders):
        named = request_at(place, order, own_rows)
        out[...] = jnp.where((named == mine) & first, 1.0, 0.0).astype(bf16)


def own_kernel(queries, new_keys, own_top):
    where = lax.broadcasted_iota(jnp.int32, own_top.shape, 1)
    top = jnp.zeros(own_top.shape, f32)
    for head in range(queries.shape[1] // HD):
        cut = slice(head * HD, (head + 1) * HD)
        score = jnp.sum(
            queries[:, cut].astype(f32) * new_keys[:, cut].astype(f32), axis=1, keepdims=True
        ) * (1.0 / math.sqrt(HD))
        top = jnp.where(where == head, score, top)
    own_top[...] = top


def split_top(top):
    lane = lax.broadcasted_iota(jnp.int32, top.shape, 1)
    top = jnp.where(lane < STAT, top, 0.0)
    high = top.astype(bf16).astype(f32)
    rest = top - high
    middle = rest.astype(bf16).astype(f32)
    low = rest - middle
    return high + pltpu.roll(middle, STAT, 1) + pltpu.roll(low, 2 * STAT, 1)


def join_top(stat):
    return (stat + pltpu.roll(stat, LANES - STAT, 1)) + pltpu.roll(stat, LANES - 2 * STAT, 1)


def stacked(refs):
    return jnp.concatenate([ref[...].astype(f32) for ref in refs], axis=0)


def pack_kernel(count, *refs):
    refs[-1][...] = stacked(refs[:count]).astype(bf16)


def hold_kernel(queries, held):
    held[...] = queries[...]


def ready_kernel(*refs):
    refs[-1][...] = jnp.zeros_like(refs[-1])


def attend_kernel(count, pick, spread_to, mask, keys, values, *refs):
    blocks, outs = refs[:count], refs[count:]
    rows = pick.shape[0]
    heads = keys.shape[1] // HD
    lane = lax.broadcasted_iota(jnp.int32, (rows, LANES), 1)
    live = mask[...] > 0.0
    chosen = jnp.dot(pick[...], stacked(blocks).astype(bf16), preferred_element_type=f32)
    zero = jnp.zeros((rows, HD), f32)
    sets = [tuple(range(at, min(at + 2, heads))) for at in range(0, heads, 2)]
    cuts = [slice(each[0] * HD, (each[-1] + 1) * HD) for each in sets]

    def diagonal(each):
        bands = [
            jnp.concatenate(
                [chosen[:, head * HD : (head + 1) * HD] if other == head else zero for other in each],
                axis=1,
            )
            for head in each
        ]
        return jnp.concatenate(bands, axis=0).astype(bf16)

    def score_of(each, cut):
        return lax.dot_general(
            diagonal(each), keys[:, cut], (((1,), (1,)), ((), ())), preferred_element_type=f32
        )

    def weigh(each, score):
        wide = jnp.concatenate([live] * len(each), axis=0)
        score = jnp.where(wide, score * (1.0 / math.sqrt(HD)), floor_score)
        top = jnp.max(score, axis=1, keepdims=True)
        weight = jnp.where(wide, jnp.exp(score - top), 0.0).astype(bf16)
        denom = jnp.sum(weight.astype(f32), axis=1, keepdims=True)
        denom = jnp.where(denom > 0.0, denom, 1.0)
        return weight, denom, top + jnp.log(denom)

    def value_of(each, cut, weight, denom):
        numer = jnp.dot(weight, values[:, cut], preferred_element_type=f32) / denom
        return [
            numer[at * rows : (at + 1) * rows, at * HD : (at + 1) * HD] for at in range(len(each))
        ]

    tops = jnp.zeros((rows, LANES), f32)
    scores, weights, found = {}, {}, []
    for step in range(len(sets) + 2 * LAG):
        if step < len(sets):
            scores[step] = score_of(sets[step], cuts[step])
        at = step - LAG
        if 0 <= at < len(sets):
            *weights[at], top = weigh(sets[at], scores.pop(at))
            for place, head in enumerate(sets[at]):
                tops = jnp.where(lane == head, top[place * rows : (place + 1) * rows], tops)
        at = step - 2 * LAG
        if 0 <= at < len(sets):
            found += value_of(sets[at], cuts[at], *weights.pop(at))
    spread = functools.partial(
        lax.dot_general, dimension_numbers=(((0,), (0,)), ((), ())), preferred_element_type=f32
    )
    dense = spread(spread_to[...], jnp.concatenate(found, axis=1).astype(bf16)).astype(bf16)
    stat = jnp.where(lane == LANES - 1, 1.0, split_top(tops)).astype(bf16)
    stat = spread(spread_to[...], stat)
    place = lax.broadcasted_iota(jnp.int32, stat.shape, 1)
    absent = stat[:, LANES - 1 :] == 0.0
    stat = jnp.where(absent & (place < STAT), floor_score, stat).astype(bf16)
    size = outs[0].shape[0]
    for at, out in enumerate(outs):
        part = slice(at * size, (at + 1) * size)
        out[:, : heads * HD] = dense[part]
        out[:, heads * HD :] = stat[part]


def merge(parts, tops):
    best = functools.reduce(jnp.maximum, tops)
    weights = [jnp.exp(top - best) for top in tops]
    total = functools.reduce(jnp.add, weights)
    shares = [weight / total for weight in weights[1:]]

    def head_of(head):
        first = parts[0](head)
        value = first
        for share, part in zip(shares, parts[1:]):
            value = value + share[:, head : head + 1] * (part(head) - first)
        return value

    return head_of, best + jnp.log(total)


def part_of(ref, start, rows):
    return lambda head: ref[:, head * HD : (head + 1) * HD].astype(f32)[start : start + rows]


def top_of(ref, start, rows):
    return join_top(ref[:, ref.shape[1] - LANES :].astype(f32)[start : start + rows])


def merge_kernel(count, *refs):
    ins, outs = refs[:count], refs[count:]
    heads = ins[0].shape[1] // HD - 1
    rows = sum(out.shape[0] for out in outs)
    head_of, top = merge(
        [part_of(ref, 0, rows) for ref in ins], [top_of(ref, 0, rows) for ref in ins]
    )
    for head in range(heads + 1):
        cut = slice(head * HD, (head + 1) * HD)
        block = head_of(head) if head < heads else split_top(top)
        at = 0
        for out in outs:
            out[:, cut] = block[at : at + out.shape[0]].astype(bf16)
            at += out.shape[0]


def last_kernel(count, *refs):
    ins = refs[:count]
    new_values, own_top, out = refs[count:]
    rows = out.shape[0]
    head_of, _ = merge(
        [part_of(ref, ref.shape[0] - rows, rows) for ref in ins] + [part_of(new_values, 0, rows)],
        [top_of(ref, ref.shape[0] - rows, rows) for ref in ins] + [own_top[...]],
    )
    for head in range(out.shape[1] // HD):
        out[:, head * HD : (head + 1) * HD] = head_of(head).astype(bf16)


def project_kernel(mid, own_rows, count, *refs):
    blocks, weight, outs, acc = refs[:count], refs[count], refs[count + 1 : -1], refs[-1]
    product = lax.dot_general(
        stacked(blocks).astype(bf16),
        weight[...],
        (((1,), (1,)), ((), ())),
        preferred_element_type=f32,
    )
    for at, distance in enumerate(gather_order(mid, RESULT_ORDER)):
        owner = lax.bitwise_xor(lax.axis_index("kv"), distance)
        start = pl.multiple_of(owner * own_rows, own_rows)
        acc[pl.ds(start, own_rows), :] = product[at * own_rows : (at + 1) * own_rows]
    for distance, out in enumerate(outs):
        rows = out.shape[0]
        side = lax.bitwise_xor(lax.axis_index("tp"), distance)
        out[...] = acc[pl.ds(pl.multiple_of(side * rows, rows), rows), :].astype(out.dtype)


def base_kernel(kept, residual, bias, total):
    total[...] = kept[...] + residual[...].astype(f32) + bias[...].astype(f32)


def final_kernel(total, *refs):
    value = total[...]
    for part in refs[:-1]:
        value = value + part[...].astype(f32)
    refs[-1][...] = value.astype(bf16)


def hop(x, axis, count, distance):
    return lax.ppermute(x, axis, [(i, i ^ distance) for i in range(count)])


def on_device(
    kv_count,
    tp_count,
    queries,
    new_keys,
    new_values,
    keys,
    values,
    slot_request,
    slot_valid,
    out_weight,
    out_bias,
    residual,
):
    own_rows, width = queries.shape
    slots = keys.shape[0]
    mid = kv_count // (2 * OUTER)
    requests = kv_count * own_rows
    rows = -(-(slots // PAGE) // 16) * 16
    wide = width + LANES
    kv_hop = lambda x, distance: hop(x, "kv", kv_count, distance)
    shaped = jax.ShapeDtypeStruct

    def call(kernel, shapes, scratch, name, *operands, spec=lambda at: WHOLE):
        single = not isinstance(shapes, tuple)
        return pl.pallas_call(
            kernel,
            out_shape=shapes,
            in_specs=[spec(at) for at in range(len(operands))],
            out_specs=WHOLE if single else (WHOLE,) * len(shapes),
            scratch_shapes=scratch,
            compiler_params=params(),
            name=name,
        )(*operands)

    def pack(parts, *after):
        return call(
            functools.partial(pack_kernel, len(parts)),
            shaped((sum(x.shape[0] for x in parts), width), bf16),
            [],
            "pack",
            *parts,
            *after,
            spec=lambda at: WHOLE if at < len(parts) else ANY,
        )

    def gather(block, own, order, before, after, beside):
        outer = {far: kv_hop(block, 2 * mid * far) for far in order}
        across = [
            kv_hop(block, 2 * middle + 2 * mid * order[2]) for middle in range(1, mid)
        ]
        relay = pack([outer[far] for far in relayed(order)] + [own], *before)
        near = pack([relay, outer[order[2]], *across], *beside)
        far = [kv_hop(relay, 2 * middle) for middle in range(1, mid)]
        if after:
            far = [pack(far, *after)]
        line = [near] + far
        return line + [kv_hop(x, 1) for x in line]

    pick, spread_to, mask = call(
        functools.partial(prep_kernel, mid, own_rows),
        (
            shaped((rows, requests), bf16),
            shaped((rows, requests), bf16),
            shaped((rows, slots), f32),
        ),
        [],
        "prep",
        slot_request.reshape(1, slots),
        slot_valid.reshape(1, slots),
    )
    held = call(hold_kernel, shaped(queries.shape, bf16), [], "hold", queries)
    own_top = call(own_kernel, shaped((own_rows, LANES), f32), [], "own", held, new_keys)
    ready = [
        call(ready_kernel, shaped((8, LANES), f32), [], "ready", x, spec=lambda at: ANY)
        for x in (keys, values)
    ]
    blocks = gather(queries, held, QUERY_ORDER, [own_top], [ready[0], pick], [ready[1]])
    size = OUTER * own_rows
    outs = call(
        functools.partial(attend_kernel, len(blocks)),
        (shaped((size, wide), bf16),) * (2 * mid),
        [],
        "attend",
        pick,
        spread_to,
        mask,
        keys,
        values,
        *blocks,
    )

    def merged(ins, *heights):
        return call(
            functools.partial(merge_kernel, len(ins)),
            tuple(shaped((height * own_rows, wide), bf16) for height in heights),
            [],
            "merge",
            *ins,
        )

    relays, ins = [], []
    for middle in range(1, mid):
        relay, straight = merged([outs[middle], kv_hop(outs[mid + middle], 1)], 3, 1)
        relays.append(kv_hop(relay, 2 * middle))
        ins.append(kv_hop(straight, 2 * middle + 2 * mid * REDUCE_ORDER[2]))
    *pair, own, straight = merged([outs[0], kv_hop(outs[mid], 1)], 2, 1, 1)
    pair = merged(pair + relays, 1, 1)
    ins += [own, *relays, kv_hop(straight, 2 * mid * REDUCE_ORDER[2])]
    ins += [kv_hop(x, 2 * mid * far) for x, far in zip(pair, relayed(REDUCE_ORDER))]
    attended = call(
        functools.partial(last_kernel, len(ins)),
        shaped((own_rows, width), bf16),
        [],
        "last",
        *ins,
        new_values,
        own_top,
    )

    blocks = gather(attended, attended, RESULT_ORDER, [], [], [])
    columns = out_weight.shape[1]
    shape = (requests // tp_count, columns)
    kept, *sent = call(
        functools.partial(project_kernel, mid, own_rows, len(blocks)),
        (shaped(shape, f32),) + (shaped(shape, SENT),) * (tp_count - 1),
        [pltpu.VMEM((requests, columns), f32)],
        "project",
        *blocks,
        out_weight.T,
    )
    received = [hop(x, "tp", tp_count, at + 1) for at, x in enumerate(sent)]
    total = call(
        base_kernel, shaped(shape, f32), [], "base", kept, residual, out_bias.reshape(1, columns)
    )
    return call(final_kernel, shaped(shape, bf16), [], "final", total, *received)


def solution(mesh):
    placed = (
        P("kv", "tp"),
        P("kv", "tp"),
        P("kv", "tp"),
        P("kv", "tp"),
        P("kv", "tp"),
        P("kv"),
        P("kv"),
        P("tp", "kv"),
        P("kv"),
        P("tp", "kv"),
    )
    return jax.shard_map(
        functools.partial(on_device, mesh.shape["kv"], mesh.shape["tp"]),
        mesh=mesh,
        in_specs=placed,
        out_specs=P("tp", "kv"),
        check_vma=False,
    )
```

```python
import functools
import math

import jax
import jax.numpy as jnp
from jax import lax
from jax.experimental import pallas as pl
from jax.experimental.pallas import tpu as pltpu
from jax.sharding import PartitionSpec as P

HD = 128
PAGE = 16
OUTER = 4
LANES = 128
LAG = 3
STAT = 32

floor_score = -1e30
SENT = jnp.bfloat16
QUERY_ORDER = (3, 2, 1)
REDUCE_ORDER = (2, 1, 3)
RESULT_ORDER = (3, 2, 1)
f32 = jnp.float32
bf16 = jnp.bfloat16
WHOLE = pl.BlockSpec(memory_space=pltpu.VMEM)
ANY = pl.BlockSpec(memory_space=pl.ANY)


def params(megabytes=24):
    return pltpu.CompilerParams(vmem_limit_bytes=megabytes * 1024 * 1024)


def relayed(order):
    return list(order[:2])


def gather_order(mid, order):
    lines = [[(far, 0) for far in relayed(order) + [0, order[2]]]]
    lines[0] += [(order[2], middle) for middle in range(1, mid)]
    lines += [[(far, middle) for far in relayed(order) + [0]] for middle in range(1, mid)]
    return [
        core + 2 * middle + 2 * mid * far
        for core in (0, 1)
        for line in lines
        for far, middle in line
    ]


def reduce_order(mid, order):
    return [
        core + 2 * middle + 2 * mid * far
        for core in (0, 1)
        for middle in range(mid)
        for far in relayed(order) + [0, order[2]]
    ]


def request_at(place, order, own_rows):
    distance = jnp.zeros_like(place)
    for at, value in enumerate(order):
        distance = jnp.where(place // own_rows == at, value, distance)
    return lax.bitwise_xor(distance, lax.axis_index("kv")) * own_rows + place % own_rows


def prep_kernel(mid, own_rows, request, valid, pick, spread, mask):
    rows, slots = mask.shape
    row = lax.broadcasted_iota(jnp.int32, (rows, slots), 0)
    lane = lax.broadcasted_iota(jnp.int32, (rows, slots), 1)
    owners = jnp.broadcast_to(request[...], (rows, slots))
    mine = jnp.sum(jnp.where(lane == row * PAGE, owners, 0), axis=1, keepdims=True)
    before = jnp.sum(jnp.where(lane == row * PAGE - PAGE, owners, 0), axis=1, keepdims=True)
    page = lax.broadcasted_iota(jnp.int32, (rows, 1), 0)
    first = ((page == 0) | (mine != before)) & (page < slots // PAGE)
    live = (owners == mine) & first & (jnp.broadcast_to(valid[...], (rows, slots)) == 1)
    mask[...] = jnp.where(live, 1.0, 0.0)
    place = lax.broadcasted_iota(jnp.int32, pick.shape, 1)
    orders = (gather_order(mid, QUERY_ORDER), reduce_order(mid, REDUCE_ORDER))
    for out, order in zip((pick, spread), orders):
        named = request_at(place, order, own_rows)
        out[...] = jnp.where((named == mine) & first, 1.0, 0.0).astype(bf16)


def own_kernel(queries, new_keys, own_top):
    where = lax.broadcasted_iota(jnp.int32, own_top.shape, 1)
    top = jnp.zeros(own_top.shape, f32)
    for head in range(queries.shape[1] // HD):
        cut = slice(head * HD, (head + 1) * HD)
        score = jnp.sum(
            queries[:, cut].astype(f32) * new_keys[:, cut].astype(f32), axis=1, keepdims=True
        ) * (1.0 / math.sqrt(HD))
        top = jnp.where(where == head, score, top)
    own_top[...] = top


def split_top(top):
    lane = lax.broadcasted_iota(jnp.int32, top.shape, 1)
    top = jnp.where(lane < STAT, top, 0.0)
    high = top.astype(bf16).astype(f32)
    rest = top - high
    middle = rest.astype(bf16).astype(f32)
    low = rest - middle
    return high + pltpu.roll(middle, STAT, 1) + pltpu.roll(low, 2 * STAT, 1)


def join_top(stat):
    return (stat + pltpu.roll(stat, LANES - STAT, 1)) + pltpu.roll(stat, LANES - 2 * STAT, 1)


def stacked(refs):
    return jnp.concatenate([ref[...].astype(f32) for ref in refs], axis=0)


def pack_kernel(count, *refs):
    refs[-1][...] = stacked(refs[:count]).astype(bf16)


def hold_kernel(queries, held):
    held[...] = queries[...]


def ready_kernel(*refs):
    refs[-1][...] = jnp.zeros_like(refs[-1])


def attend_kernel(count, pick, spread_to, mask, keys, values, *refs):
    blocks, outs = refs[:count], refs[count:]
    rows = pick.shape[0]
    heads = keys.shape[1] // HD
    lane = lax.broadcasted_iota(jnp.int32, (rows, LANES), 1)
    live = mask[...] > 0.0
    chosen = jnp.dot(pick[...], stacked(blocks).astype(bf16), preferred_element_type=f32)
    zero = jnp.zeros((rows, HD), f32)
    sets = [tuple(range(at, min(at + 2, heads))) for at in range(0, heads, 2)]
    cuts = [slice(each[0] * HD, (each[-1] + 1) * HD) for each in sets]

    def diagonal(each):
        bands = [
            jnp.concatenate(
                [chosen[:, head * HD : (head + 1) * HD] if other == head else zero for other in each],
                axis=1,
            )
            for head in each
        ]
        return jnp.concatenate(bands, axis=0).astype(bf16)

    def score_of(each, cut):
        return lax.dot_general(
            diagonal(each), keys[:, cut], (((1,), (1,)), ((), ())), preferred_element_type=f32
        )

    def weigh(each, score):
        wide = jnp.concatenate([live] * len(each), axis=0)
        score = jnp.where(wide, score * (1.0 / math.sqrt(HD)), floor_score)
        top = jnp.max(score, axis=1, keepdims=True)
        weight = jnp.exp(score - jnp.where(top > floor_score, top, 0.0)).astype(bf16)
        denom = jnp.sum(weight.astype(f32), axis=1, keepdims=True)
        denom = jnp.where(denom > 0.0, denom, 1.0)
        return weight, denom, top + jnp.log(denom)

    def value_of(each, cut, weight, denom):
        numer = jnp.dot(weight, values[:, cut], preferred_element_type=f32) / denom
        return [
            numer[at * rows : (at + 1) * rows, at * HD : (at + 1) * HD] for at in range(len(each))
        ]

    tops = jnp.zeros((rows, LANES), f32)
    scores, weights, found = {}, {}, []
    for step in range(len(sets) + 2 * LAG):
        if step < len(sets):
            scores[step] = score_of(sets[step], cuts[step])
        at = step - LAG
        if 0 <= at < len(sets):
            *weights[at], top = weigh(sets[at], scores.pop(at))
            for place, head in enumerate(sets[at]):
                tops = jnp.where(lane == head, top[place * rows : (place + 1) * rows], tops)
        at = step - 2 * LAG
        if 0 <= at < len(sets):
            found += value_of(sets[at], cuts[at], *weights.pop(at))
    spread = functools.partial(
        lax.dot_general, dimension_numbers=(((0,), (0,)), ((), ())), preferred_element_type=f32
    )
    dense = spread(spread_to[...], jnp.concatenate(found, axis=1).astype(bf16)).astype(bf16)
    stat = jnp.where(lane == LANES - 1, 1.0, split_top(tops)).astype(bf16)
    stat = spread(spread_to[...], stat)
    place = lax.broadcasted_iota(jnp.int32, stat.shape, 1)
    absent = stat[:, LANES - 1 :] == 0.0
    stat = jnp.where(absent & (place < STAT), floor_score, stat).astype(bf16)
    size = outs[0].shape[0]
    for at, out in enumerate(outs):
        part = slice(at * size, (at + 1) * size)
        out[:, : heads * HD] = dense[part]
        out[:, heads * HD :] = stat[part]


def merge(parts, tops):
    best = functools.reduce(jnp.maximum, tops)
    weights = [jnp.exp(top - best) for top in tops]
    total = functools.reduce(jnp.add, weights)
    shares = [weight / total for weight in weights[1:]]

    def head_of(head):
        first = parts[0](head)
        value = first
        for share, part in zip(shares, parts[1:]):
            value = value + share[:, head : head + 1] * (part(head) - first)
        return value

    return head_of, best + jnp.log(total)


def part_of(ref, start, rows):
    return lambda head: ref[:, head * HD : (head + 1) * HD].astype(f32)[start : start + rows]


def top_of(ref, start, rows):
    return join_top(ref[:, ref.shape[1] - LANES :].astype(f32)[start : start + rows])


def merge_kernel(count, *refs):
    ins, outs = refs[:count], refs[count:]
    heads = ins[0].shape[1] // HD - 1
    rows = sum(out.shape[0] for out in outs)
    head_of, top = merge(
        [part_of(ref, 0, rows) for ref in ins], [top_of(ref, 0, rows) for ref in ins]
    )
    for head in range(heads + 1):
        cut = slice(head * HD, (head + 1) * HD)
        block = head_of(head) if head < heads else split_top(top)
        at = 0
        for out in outs:
            out[:, cut] = block[at : at + out.shape[0]].astype(bf16)
            at += out.shape[0]


def early_kernel(count, *refs):
    ins = refs[:count]
    new_values, own_top, out = refs[count:]
    rows = out.shape[0]
    heads = new_values.shape[1] // HD
    head_of, top = merge(
        [part_of(ref, ref.shape[0] - rows, rows) for ref in ins] + [part_of(new_values, 0, rows)],
        [top_of(ref, ref.shape[0] - rows, rows) for ref in ins] + [own_top[...]],
    )
    for head in range(heads):
        out[:, head * HD : (head + 1) * HD] = head_of(head)
    out[:, heads * HD :] = top


def last_kernel(count, *refs):
    ins, early, out = refs[:count], refs[count], refs[count + 1]
    rows, width = out.shape
    head_of, _ = merge(
        [part_of(early, 0, rows)] + [part_of(ref, 0, rows) for ref in ins],
        [early[:, width:]] + [top_of(ref, 0, rows) for ref in ins],
    )
    for head in range(width // HD):
        out[:, head * HD : (head + 1) * HD] = head_of(head).astype(bf16)


def project_kernel(mid, own_rows, count, *refs):
    blocks, weight, outs, acc = refs[:count], refs[count], refs[count + 1 : -1], refs[-1]
    product = lax.dot_general(
        stacked(blocks).astype(bf16),
        weight[...],
        (((1,), (1,)), ((), ())),
        preferred_element_type=f32,
    )
    for at, distance in enumerate(gather_order(mid, RESULT_ORDER)):
        owner = lax.bitwise_xor(lax.axis_index("kv"), distance)
        start = pl.multiple_of(owner * own_rows, own_rows)
        acc[pl.ds(start, own_rows), :] = product[at * own_rows : (at + 1) * own_rows]
    for distance, out in enumerate(outs):
        rows = out.shape[0]
        side = lax.bitwise_xor(lax.axis_index("tp"), distance)
        out[...] = acc[pl.ds(pl.multiple_of(side * rows, rows), rows), :].astype(out.dtype)


def base_kernel(kept, residual, bias, total):
    total[...] = kept[...] + residual[...].astype(f32) + bias[...].astype(f32)


def final_kernel(total, *refs):
    value = total[...]
    for part in refs[:-1]:
        value = value + part[...].astype(f32)
    refs[-1][...] = value.astype(bf16)


def hop(x, axis, count, distance):
    return lax.ppermute(x, axis, [(i, i ^ distance) for i in range(count)])


def on_device(
    kv_count,
    tp_count,
    queries,
    new_keys,
    new_values,
    keys,
    values,
    slot_request,
    slot_valid,
    out_weight,
    out_bias,
    residual,
):
    own_rows, width = queries.shape
    slots = keys.shape[0]
    mid = kv_count // (2 * OUTER)
    requests = kv_count * own_rows
    rows = -(-(slots // PAGE) // 16) * 16
    wide = width + LANES
    kv_hop = lambda x, distance: hop(x, "kv", kv_count, distance)
    shaped = jax.ShapeDtypeStruct

    def call(kernel, shapes, scratch, name, *operands, spec=lambda at: WHOLE):
        single = not isinstance(shapes, tuple)
        return pl.pallas_call(
            kernel,
            out_shape=shapes,
            in_specs=[spec(at) for at in range(len(operands))],
            out_specs=WHOLE if single else (WHOLE,) * len(shapes),
            scratch_shapes=scratch,
            compiler_params=params(),
            name=name,
        )(*operands)

    def pack(parts, *after):
        return call(
            functools.partial(pack_kernel, len(parts)),
            shaped((sum(x.shape[0] for x in parts), width), bf16),
            [],
            "pack",
            *parts,
            *after,
            spec=lambda at: WHOLE if at < len(parts) else ANY,
        )

    def gather(block, own, order, before, after, beside):
        outer = {far: kv_hop(block, 2 * mid * far) for far in order}
        across = [
            kv_hop(block, 2 * middle + 2 * mid * order[2]) for middle in range(1, mid)
        ]
        relay = pack([outer[far] for far in relayed(order)] + [own], *before)
        near = pack([relay, outer[order[2]], *across], *beside)
        far = [kv_hop(relay, 2 * middle) for middle in range(1, mid)]
        if after:
            far = [pack(far, *after)]
        line = [near] + far
        return line + [kv_hop(x, 1) for x in line]

    pick, spread_to, mask = call(
        functools.partial(prep_kernel, mid, own_rows),
        (
            shaped((rows, requests), bf16),
            shaped((rows, requests), bf16),
            shaped((rows, slots), f32),
        ),
        [],
        "prep",
        slot_request.reshape(1, slots),
        slot_valid.reshape(1, slots),
    )
    held = call(hold_kernel, shaped(queries.shape, bf16), [], "hold", queries)
    own_top = call(own_kernel, shaped((own_rows, LANES), f32), [], "own", held, new_keys)
    ready = [
        call(ready_kernel, shaped((8, LANES), f32), [], "ready", x, spec=lambda at: ANY)
        for x in (keys, values)
    ]
    blocks = gather(queries, held, QUERY_ORDER, [own_top], [ready[0], pick], [ready[1]])
    size = OUTER * own_rows
    outs = call(
        functools.partial(attend_kernel, len(blocks)),
        (shaped((size, wide), bf16),) * (2 * mid),
        [],
        "attend",
        pick,
        spread_to,
        mask,
        keys,
        values,
        *blocks,
    )

    def merged(ins, *heights):
        return call(
            functools.partial(merge_kernel, len(ins)),
            tuple(shaped((height * own_rows, wide), bf16) for height in heights),
            [],
            "merge",
            *ins,
        )

    relays, ins = [], []
    for middle in range(1, mid):
        relay, straight = merged([outs[middle], kv_hop(outs[mid + middle], 1)], 3, 1)
        relays.append(kv_hop(relay, 2 * middle))
        ins.append(kv_hop(straight, 2 * middle + 2 * mid * REDUCE_ORDER[2]))
    *pair, own, straight = merged([outs[0], kv_hop(outs[mid], 1)], 2, 1, 1)
    pair = merged(pair + relays, 1, 1)
    ins += [own, *relays, kv_hop(straight, 2 * mid * REDUCE_ORDER[2])]
    early = call(
        functools.partial(early_kernel, len(ins)),
        shaped((own_rows, wide), f32),
        [],
        "early",
        *ins,
        new_values,
        own_top,
    )
    ins = [kv_hop(x, 2 * mid * far) for x, far in zip(pair, relayed(REDUCE_ORDER))]
    attended = call(
        functools.partial(last_kernel, len(ins)),
        shaped((own_rows, width), bf16),
        [],
        "last",
        *ins,
        early,
    )

    blocks = gather(attended, attended, RESULT_ORDER, [], [], [])
    columns = out_weight.shape[1]
    shape = (requests // tp_count, columns)
    kept, *sent = call(
        functools.partial(project_kernel, mid, own_rows, len(blocks)),
        (shaped(shape, f32),) + (shaped(shape, SENT),) * (tp_count - 1),
        [pltpu.VMEM((requests, columns), f32)],
        "project",
        *blocks,
        out_weight.T,
    )
    received = [hop(x, "tp", tp_count, at + 1) for at, x in enumerate(sent)]
    total = call(
        base_kernel, shaped(shape, f32), [], "base", kept, residual, out_bias.reshape(1, columns)
    )
    return call(final_kernel, shaped(shape, bf16), [], "final", total, *received)


def solution(mesh):
    placed = (
        P("kv", "tp"),
        P("kv", "tp"),
        P("kv", "tp"),
        P("kv", "tp"),
        P("kv", "tp"),
        P("kv"),
        P("kv"),
        P("tp", "kv"),
        P("kv"),
        P("tp", "kv"),
    )
    return jax.shard_map(
        functools.partial(on_device, mesh.shape["kv"], mesh.shape["tp"]),
        mesh=mesh,
        in_specs=placed,
        out_specs=P("tp", "kv"),
        check_vma=False,
    )
```

```python
import functools
import math

import jax
import jax.numpy as jnp
from jax import lax
from jax.experimental import pallas as pl
from jax.experimental.pallas import tpu as pltpu
from jax.sharding import PartitionSpec as P

HD = 128
PAGE = 16
OUTER = 4
LANES = 128
LAG = 4
STAT = 32

floor_score = -1e30
SENT = jnp.bfloat16
QUERY_ORDER = (3, 2, 1)
REDUCE_ORDER = (2, 1, 3)
RESULT_ORDER = (3, 2, 1)
f32 = jnp.float32
bf16 = jnp.bfloat16
WHOLE = pl.BlockSpec(memory_space=pltpu.VMEM)
ANY = pl.BlockSpec(memory_space=pl.ANY)


def params(megabytes=24):
    return pltpu.CompilerParams(vmem_limit_bytes=megabytes * 1024 * 1024)


def relayed(order):
    return list(order[:2])


def gather_order(mid, order):
    lines = [[(far, 0) for far in relayed(order) + [0, order[2]]]]
    lines[0] += [(order[2], middle) for middle in range(1, mid)]
    lines += [[(far, middle) for far in relayed(order) + [0]] for middle in range(1, mid)]
    return [
        core + 2 * middle + 2 * mid * far
        for core in (0, 1)
        for line in lines
        for far, middle in line
    ]


def reduce_order(mid, order):
    return [
        core + 2 * middle + 2 * mid * far
        for core in (0, 1)
        for middle in range(mid)
        for far in relayed(order) + [0, order[2]]
    ]


def request_at(place, order, own_rows):
    distance = jnp.zeros_like(place)
    for at, value in enumerate(order):
        distance = jnp.where(place // own_rows == at, value, distance)
    return lax.bitwise_xor(distance, lax.axis_index("kv")) * own_rows + place % own_rows


def prep_kernel(mid, own_rows, request, valid, pick, spread, mask):
    rows, slots = mask.shape
    row = lax.broadcasted_iota(jnp.int32, (rows, slots), 0)
    lane = lax.broadcasted_iota(jnp.int32, (rows, slots), 1)
    owners = jnp.broadcast_to(request[...], (rows, slots))
    mine = jnp.sum(jnp.where(lane == row * PAGE, owners, 0), axis=1, keepdims=True)
    before = jnp.sum(jnp.where(lane == row * PAGE - PAGE, owners, 0), axis=1, keepdims=True)
    page = lax.broadcasted_iota(jnp.int32, (rows, 1), 0)
    first = ((page == 0) | (mine != before)) & (page < slots // PAGE)
    live = (owners == mine) & first & (jnp.broadcast_to(valid[...], (rows, slots)) == 1)
    mask[...] = jnp.where(live, 1.0, 0.0)
    place = lax.broadcasted_iota(jnp.int32, pick.shape, 1)
    orders = (gather_order(mid, QUERY_ORDER), reduce_order(mid, REDUCE_ORDER))
    for out, order in zip((pick, spread), orders):
        named = request_at(place, order, own_rows)
        out[...] = jnp.where((named == mine) & first, 1.0, 0.0).astype(bf16)


def own_kernel(queries, new_keys, own_top):
    where = lax.broadcasted_iota(jnp.int32, own_top.shape, 1)
    top = jnp.zeros(own_top.shape, f32)
    for head in range(queries.shape[1] // HD):
        cut = slice(head * HD, (head + 1) * HD)
        score = jnp.sum(
            queries[:, cut].astype(f32) * new_keys[:, cut].astype(f32), axis=1, keepdims=True
        ) * (1.0 / math.sqrt(HD))
        top = jnp.where(where == head, score, top)
    own_top[...] = top


def split_top(top):
    lane = lax.broadcasted_iota(jnp.int32, top.shape, 1)
    top = jnp.where(lane < STAT, top, 0.0)
    high = top.astype(bf16).astype(f32)
    rest = top - high
    middle = rest.astype(bf16).astype(f32)
    low = rest - middle
    return high + pltpu.roll(middle, STAT, 1) + pltpu.roll(low, 2 * STAT, 1)


def join_top(stat):
    return (stat + pltpu.roll(stat, LANES - STAT, 1)) + pltpu.roll(stat, LANES - 2 * STAT, 1)


def stacked(refs):
    return jnp.concatenate([ref[...].astype(f32) for ref in refs], axis=0)


def pack_kernel(count, *refs):
    refs[-1][...] = stacked(refs[:count]).astype(bf16)


def hold_kernel(queries, held):
    held[...] = queries[...]


def ready_kernel(*refs):
    refs[-1][...] = jnp.zeros_like(refs[-1])


def attend_kernel(count, pick, spread_to, mask, keys, values, *refs):
    blocks, outs = refs[:count], refs[count:]
    rows = pick.shape[0]
    heads = keys.shape[1] // HD
    lane = lax.broadcasted_iota(jnp.int32, (rows, LANES), 1)
    live = mask[...] > 0.0
    chosen = jnp.dot(pick[...], stacked(blocks).astype(bf16), preferred_element_type=f32)
    zero = jnp.zeros((rows, HD), f32)
    sets = [tuple(range(at, min(at + 2, heads))) for at in range(0, heads, 2)]
    cuts = [slice(each[0] * HD, (each[-1] + 1) * HD) for each in sets]

    def diagonal(each):
        bands = [
            jnp.concatenate(
                [chosen[:, head * HD : (head + 1) * HD] if other == head else zero for other in each],
                axis=1,
            )
            for head in each
        ]
        return jnp.concatenate(bands, axis=0).astype(bf16)

    def score_of(each, cut):
        return lax.dot_general(
            diagonal(each), keys[:, cut], (((1,), (1,)), ((), ())), preferred_element_type=f32
        )

    def weigh(each, score):
        wide = jnp.concatenate([live] * len(each), axis=0)
        score = jnp.where(wide, score * (1.0 / math.sqrt(HD)), floor_score)
        top = jnp.max(score, axis=1, keepdims=True)
        weight = jnp.exp(score - jnp.where(top > floor_score, top, 0.0)).astype(bf16)
        denom = jnp.sum(weight.astype(f32), axis=1, keepdims=True)
        denom = jnp.where(denom > 0.0, denom, 1.0)
        return weight, denom, top + jnp.log(denom)

    def value_of(each, cut, weight, denom):
        numer = jnp.dot(weight, values[:, cut], preferred_element_type=f32) / denom
        return [
            numer[at * rows : (at + 1) * rows, at * HD : (at + 1) * HD] for at in range(len(each))
        ]

    tops = jnp.zeros((rows, LANES), f32)
    scores, weights, found = {}, {}, []
    for step in range(len(sets) + 2 * LAG):
        if step < len(sets):
            scores[step] = score_of(sets[step], cuts[step])
        at = step - LAG
        if 0 <= at < len(sets):
            *weights[at], top = weigh(sets[at], scores.pop(at))
            for place, head in enumerate(sets[at]):
                tops = jnp.where(lane == head, top[place * rows : (place + 1) * rows], tops)
        at = step - 2 * LAG
        if 0 <= at < len(sets):
            found += value_of(sets[at], cuts[at], *weights.pop(at))
    spread = functools.partial(
        lax.dot_general, dimension_numbers=(((0,), (0,)), ((), ())), preferred_element_type=f32
    )
    dense = spread(spread_to[...], jnp.concatenate(found, axis=1).astype(bf16)).astype(bf16)
    stat = jnp.where(lane == LANES - 1, 1.0, split_top(tops)).astype(bf16)
    stat = spread(spread_to[...], stat)
    place = lax.broadcasted_iota(jnp.int32, stat.shape, 1)
    absent = stat[:, LANES - 1 :] == 0.0
    stat = jnp.where(absent & (place < STAT), floor_score, stat).astype(bf16)
    size = outs[0].shape[0]
    for at, out in enumerate(outs):
        part = slice(at * size, (at + 1) * size)
        out[:, : heads * HD] = dense[part]
        out[:, heads * HD :] = stat[part]


def merge(parts, tops):
    best = functools.reduce(jnp.maximum, tops)
    weights = [jnp.exp(top - best) for top in tops]
    total = functools.reduce(jnp.add, weights)
    shares = [weight / total for weight in weights[1:]]

    def head_of(head):
        first = parts[0](head)
        value = first
        for share, part in zip(shares, parts[1:]):
            value = value + share[:, head : head + 1] * (part(head) - first)
        return value

    return head_of, best + jnp.log(total)


def part_of(ref, start, rows):
    return lambda head: ref[:, head * HD : (head + 1) * HD].astype(f32)[start : start + rows]


def top_of(ref, start, rows):
    return join_top(ref[:, ref.shape[1] - LANES :].astype(f32)[start : start + rows])


def merge_kernel(count, *refs):
    ins, outs = refs[:count], refs[count:]
    heads = ins[0].shape[1] // HD - 1
    rows = sum(out.shape[0] for out in outs)
    head_of, top = merge(
        [part_of(ref, 0, rows) for ref in ins], [top_of(ref, 0, rows) for ref in ins]
    )
    for head in range(heads + 1):
        cut = slice(head * HD, (head + 1) * HD)
        block = head_of(head) if head < heads else split_top(top)
        at = 0
        for out in outs:
            out[:, cut] = block[at : at + out.shape[0]].astype(bf16)
            at += out.shape[0]


def early_kernel(count, *refs):
    ins = refs[:count]
    new_values, own_top, out = refs[count:]
    rows = out.shape[0]
    heads = new_values.shape[1] // HD
    head_of, top = merge(
        [part_of(ref, ref.shape[0] - rows, rows) for ref in ins] + [part_of(new_values, 0, rows)],
        [top_of(ref, ref.shape[0] - rows, rows) for ref in ins] + [own_top[...]],
    )
    for head in range(heads):
        out[:, head * HD : (head + 1) * HD] = head_of(head)
    out[:, heads * HD :] = top


def last_kernel(count, *refs):
    ins, early, out = refs[:count], refs[count], refs[count + 1]
    rows, width = out.shape
    head_of, _ = merge(
        [part_of(early, 0, rows)] + [part_of(ref, 0, rows) for ref in ins],
        [early[:, width:]] + [top_of(ref, 0, rows) for ref in ins],
    )
    for head in range(width // HD):
        out[:, head * HD : (head + 1) * HD] = head_of(head).astype(bf16)


def project_kernel(mid, own_rows, count, *refs):
    blocks, weight, outs, acc = refs[:count], refs[count], refs[count + 1 : -1], refs[-1]
    product = lax.dot_general(
        stacked(blocks).astype(bf16),
        weight[...],
        (((1,), (1,)), ((), ())),
        preferred_element_type=f32,
    )
    for at, distance in enumerate(gather_order(mid, RESULT_ORDER)):
        owner = lax.bitwise_xor(lax.axis_index("kv"), distance)
        start = pl.multiple_of(owner * own_rows, own_rows)
        acc[pl.ds(start, own_rows), :] = product[at * own_rows : (at + 1) * own_rows]
    for distance, out in enumerate(outs):
        rows = out.shape[0]
        side = lax.bitwise_xor(lax.axis_index("tp"), distance)
        out[...] = acc[pl.ds(pl.multiple_of(side * rows, rows), rows), :].astype(out.dtype)


def base_kernel(kept, residual, bias, total):
    total[...] = kept[...] + residual[...].astype(f32) + bias[...].astype(f32)


def final_kernel(total, *refs):
    value = total[...]
    for part in refs[:-1]:
        value = value + part[...].astype(f32)
    refs[-1][...] = value.astype(bf16)


def hop(x, axis, count, distance):
    return lax.ppermute(x, axis, [(i, i ^ distance) for i in range(count)])


def on_device(
    kv_count,
    tp_count,
    queries,
    new_keys,
    new_values,
    keys,
    values,
    slot_request,
    slot_valid,
    out_weight,
    out_bias,
    residual,
):
    own_rows, width = queries.shape
    slots = keys.shape[0]
    mid = kv_count // (2 * OUTER)
    requests = kv_count * own_rows
    rows = -(-(slots // PAGE) // 16) * 16
    wide = width + LANES
    kv_hop = lambda x, distance: hop(x, "kv", kv_count, distance)
    shaped = jax.ShapeDtypeStruct

    def call(kernel, shapes, scratch, name, *operands, spec=lambda at: WHOLE):
        single = not isinstance(shapes, tuple)
        return pl.pallas_call(
            kernel,
            out_shape=shapes,
            in_specs=[spec(at) for at in range(len(operands))],
            out_specs=WHOLE if single else (WHOLE,) * len(shapes),
            scratch_shapes=scratch,
            compiler_params=params(),
            name=name,
        )(*operands)

    def pack(parts, *after):
        return call(
            functools.partial(pack_kernel, len(parts)),
            shaped((sum(x.shape[0] for x in parts), width), bf16),
            [],
            "pack",
            *parts,
            *after,
            spec=lambda at: WHOLE if at < len(parts) else ANY,
        )

    def gather(block, own, order, before, after, beside):
        outer = {far: kv_hop(block, 2 * mid * far) for far in order}
        across = [
            kv_hop(block, 2 * middle + 2 * mid * order[2]) for middle in range(1, mid)
        ]
        relay = pack([outer[far] for far in relayed(order)] + [own], *before)
        near = pack([relay, outer[order[2]], *across], *beside)
        far = [kv_hop(relay, 2 * middle) for middle in range(1, mid)]
        if after:
            far = [pack(far, *after)]
        line = [near] + far
        return line + [kv_hop(x, 1) for x in line]

    pick, spread_to, mask = call(
        functools.partial(prep_kernel, mid, own_rows),
        (
            shaped((rows, requests), bf16),
            shaped((rows, requests), bf16),
            shaped((rows, slots), f32),
        ),
        [],
        "prep",
        slot_request.reshape(1, slots),
        slot_valid.reshape(1, slots),
    )
    held = call(hold_kernel, shaped(queries.shape, bf16), [], "hold", queries)
    own_top = call(own_kernel, shaped((own_rows, LANES), f32), [], "own", held, new_keys)
    ready = [
        call(ready_kernel, shaped((8, LANES), f32), [], "ready", x, spec=lambda at: ANY)
        for x in (keys, values)
    ]
    blocks = gather(queries, held, QUERY_ORDER, [own_top], [ready[0], pick], [ready[1]])
    size = OUTER * own_rows
    outs = call(
        functools.partial(attend_kernel, len(blocks)),
        (shaped((size, wide), bf16),) * (2 * mid),
        [],
        "attend",
        pick,
        spread_to,
        mask,
        keys,
        values,
        *blocks,
    )

    def merged(ins, *heights):
        return call(
            functools.partial(merge_kernel, len(ins)),
            tuple(shaped((height * own_rows, wide), bf16) for height in heights),
            [],
            "merge",
            *ins,
        )

    relays, ins = [], []
    for middle in range(1, mid):
        relay, straight = merged([outs[middle], kv_hop(outs[mid + middle], 1)], 3, 1)
        relays.append(kv_hop(relay, 2 * middle))
        ins.append(kv_hop(straight, 2 * middle + 2 * mid * REDUCE_ORDER[2]))
    *pair, own, straight = merged([outs[0], kv_hop(outs[mid], 1)], 2, 1, 1)
    pair = merged(pair + relays, 1, 1)
    ins += [own, *relays, kv_hop(straight, 2 * mid * REDUCE_ORDER[2])]
    early = call(
        functools.partial(early_kernel, len(ins)),
        shaped((own_rows, wide), f32),
        [],
        "early",
        *ins,
        new_values,
        own_top,
    )
    ins = [kv_hop(x, 2 * mid * far) for x, far in zip(pair, relayed(REDUCE_ORDER))]
    attended = call(
        functools.partial(last_kernel, len(ins)),
        shaped((own_rows, width), bf16),
        [],
        "last",
        *ins,
        early,
    )

    blocks = gather(attended, attended, RESULT_ORDER, [], [], [])
    columns = out_weight.shape[1]
    shape = (requests // tp_count, columns)
    kept, *sent = call(
        functools.partial(project_kernel, mid, own_rows, len(blocks)),
        (shaped(shape, f32),) + (shaped(shape, SENT),) * (tp_count - 1),
        [pltpu.VMEM((requests, columns), f32)],
        "project",
        *blocks,
        out_weight.T,
    )
    received = [hop(x, "tp", tp_count, at + 1) for at, x in enumerate(sent)]
    total = call(
        base_kernel, shaped(shape, f32), [], "base", kept, residual, out_bias.reshape(1, columns)
    )
    return call(final_kernel, shaped(shape, bf16), [], "final", total, *received)


def solution(mesh):
    placed = (
        P("kv", "tp"),
        P("kv", "tp"),
        P("kv", "tp"),
        P("kv", "tp"),
        P("kv", "tp"),
        P("kv"),
        P("kv"),
        P("tp", "kv"),
        P("kv"),
        P("tp", "kv"),
    )
    return jax.shard_map(
        functools.partial(on_device, mesh.shape["kv"], mesh.shape["tp"]),
        mesh=mesh,
        in_specs=placed,
        out_specs=P("tp", "kv"),
        check_vma=False,
    )
```

```python
import functools
import math

import jax
import jax.numpy as jnp
from jax import lax
from jax.experimental import pallas as pl
from jax.experimental.pallas import tpu as pltpu
from jax.sharding import PartitionSpec as P

HD = 128
PAGE = 16
OUTER = 4
LANES = 128
LAG = 3
STAT = 32

floor_score = -1e30
SENT = jnp.bfloat16
QUERY_ORDER = (3, 2, 1)
REDUCE_ORDER = (2, 1, 3)
RESULT_ORDER = (3, 2, 1)
f32 = jnp.float32
bf16 = jnp.bfloat16
WHOLE = pl.BlockSpec(memory_space=pltpu.VMEM)
ANY = pl.BlockSpec(memory_space=pl.ANY)


def params(megabytes=24):
    return pltpu.CompilerParams(vmem_limit_bytes=megabytes * 1024 * 1024)


def relayed(order):
    return list(order[:2])


def gather_order(mid, order):
    lines = [[(far, 0) for far in relayed(order) + [0, order[2]]]]
    lines[0] += [(order[2], middle) for middle in range(1, mid)]
    lines += [[(far, middle) for far in relayed(order) + [0]] for middle in range(1, mid)]
    return [
        core + 2 * middle + 2 * mid * far
        for core in (0, 1)
        for line in lines
        for far, middle in line
    ]


def reduce_order(mid, order):
    return [
        core + 2 * middle + 2 * mid * far
        for core in (0, 1)
        for middle in range(mid)
        for far in relayed(order) + [0, order[2]]
    ]


def request_at(place, order, own_rows):
    distance = jnp.zeros_like(place)
    for at, value in enumerate(order):
        distance = jnp.where(place // own_rows == at, value, distance)
    return lax.bitwise_xor(distance, lax.axis_index("kv")) * own_rows + place % own_rows


def prep_kernel(mid, own_rows, request, valid, pick, spread, mask):
    rows, slots = mask.shape
    row = lax.broadcasted_iota(jnp.int32, (rows, slots), 0)
    lane = lax.broadcasted_iota(jnp.int32, (rows, slots), 1)
    owners = jnp.broadcast_to(request[...], (rows, slots))
    mine = jnp.sum(jnp.where(lane == row * PAGE, owners, 0), axis=1, keepdims=True)
    before = jnp.sum(jnp.where(lane == row * PAGE - PAGE, owners, 0), axis=1, keepdims=True)
    page = lax.broadcasted_iota(jnp.int32, (rows, 1), 0)
    first = ((page == 0) | (mine != before)) & (page < slots // PAGE)
    live = (owners == mine) & first & (jnp.broadcast_to(valid[...], (rows, slots)) == 1)
    mask[...] = jnp.where(live, 1.0, 0.0)
    place = lax.broadcasted_iota(jnp.int32, pick.shape, 1)
    orders = (gather_order(mid, QUERY_ORDER), reduce_order(mid, REDUCE_ORDER))
    for out, order in zip((pick, spread), orders):
        named = request_at(place, order, own_rows)
        out[...] = jnp.where((named == mine) & first, 1.0, 0.0).astype(bf16)


def own_kernel(queries, new_keys, own_top):
    where = lax.broadcasted_iota(jnp.int32, own_top.shape, 1)
    top = jnp.zeros(own_top.shape, f32)
    for head in range(queries.shape[1] // HD):
        cut = slice(head * HD, (head + 1) * HD)
        score = jnp.sum(
            queries[:, cut].astype(f32) * new_keys[:, cut].astype(f32), axis=1, keepdims=True
        ) * (1.0 / math.sqrt(HD))
        top = jnp.where(where == head, score, top)
    own_top[...] = top


def split_top(top):
    lane = lax.broadcasted_iota(jnp.int32, top.shape, 1)
    top = jnp.where(lane < STAT, top, 0.0)
    high = top.astype(bf16).astype(f32)
    rest = top - high
    middle = rest.astype(bf16).astype(f32)
    low = rest - middle
    return high + pltpu.roll(middle, STAT, 1) + pltpu.roll(low, 2 * STAT, 1)


def join_top(stat):
    return (stat + pltpu.roll(stat, LANES - STAT, 1)) + pltpu.roll(stat, LANES - 2 * STAT, 1)


def stacked(refs):
    return jnp.concatenate([ref[...].astype(f32) for ref in refs], axis=0)


def pack_kernel(count, *refs):
    refs[-1][...] = stacked(refs[:count]).astype(bf16)


def hold_kernel(queries, held):
    held[...] = queries[...]


def ready_kernel(*refs):
    refs[-1][...] = jnp.zeros_like(refs[-1])


def attend_kernel(count, pick, spread_to, mask, keys, values, *refs):
    blocks, outs = refs[:count], refs[count:]
    rows = pick.shape[0]
    heads = keys.shape[1] // HD
    lane = lax.broadcasted_iota(jnp.int32, (rows, LANES), 1)
    live = mask[...] > 0.0
    chosen = jnp.dot(pick[...], stacked(blocks).astype(bf16), preferred_element_type=f32)
    zero = jnp.zeros((rows, HD), f32)
    sets = [tuple(range(at, min(at + 2, heads))) for at in range(0, heads, 2)]
    cuts = [slice(each[0] * HD, (each[-1] + 1) * HD) for each in sets]

    def diagonal(each):
        bands = [
            jnp.concatenate(
                [chosen[:, head * HD : (head + 1) * HD] if other == head else zero for other in each],
                axis=1,
            )
            for head in each
        ]
        return jnp.concatenate(bands, axis=0).astype(bf16)

    def score_of(each, cut):
        return lax.dot_general(
            diagonal(each), keys[:, cut], (((1,), (1,)), ((), ())), preferred_element_type=f32
        )

    def weigh(each, score):
        wide = jnp.concatenate([live] * len(each), axis=0)
        score = jnp.where(wide, score * (1.0 / math.sqrt(HD)), floor_score)
        top = jnp.max(score, axis=1, keepdims=True)
        weight = jnp.exp(score - jnp.where(top > floor_score, top, 0.0)).astype(bf16)
        denom = jnp.sum(weight.astype(f32), axis=1, keepdims=True)
        denom = jnp.where(denom > 0.0, denom, 1.0)
        return weight, denom, top + jnp.log(denom)

    def value_of(each, cut, weight, denom):
        numer = jnp.dot(weight, values[:, cut], preferred_element_type=f32) / denom
        return [
            numer[at * rows : (at + 1) * rows, at * HD : (at + 1) * HD] for at in range(len(each))
        ]

    tops = jnp.zeros((rows, LANES), f32)
    scores, weights, found = {}, {}, []
    for step in range(len(sets) + 2 * LAG):
        if step < len(sets):
            scores[step] = score_of(sets[step], cuts[step])
        at = step - LAG
        if 0 <= at < len(sets):
            *weights[at], top = weigh(sets[at], scores.pop(at))
            for place, head in enumerate(sets[at]):
                tops = jnp.where(lane == head, top[place * rows : (place + 1) * rows], tops)
        at = step - 2 * LAG
        if 0 <= at < len(sets):
            found += value_of(sets[at], cuts[at], *weights.pop(at))
    spread = functools.partial(
        lax.dot_general, dimension_numbers=(((0,), (0,)), ((), ())), preferred_element_type=f32
    )
    dense = spread(spread_to[...], jnp.concatenate(found, axis=1).astype(bf16)).astype(bf16)
    stat = jnp.where(lane == LANES - 1, 1.0, split_top(tops)).astype(bf16)
    stat = spread(spread_to[...], stat)
    place = lax.broadcasted_iota(jnp.int32, stat.shape, 1)
    absent = stat[:, LANES - 1 :] == 0.0
    stat = jnp.where(absent & (place < STAT), floor_score, stat).astype(bf16)
    size = outs[0].shape[0]
    for at, out in enumerate(outs):
        part = slice(at * size, (at + 1) * size)
        out[:, : heads * HD] = dense[part]
        out[:, heads * HD :] = stat[part]


def merge(parts, tops):
    best = functools.reduce(jnp.maximum, tops)
    weights = [jnp.exp(top - best) for top in tops]
    total = functools.reduce(jnp.add, weights)
    shares = [weight / total for weight in weights[1:]]

    def head_of(head):
        first = parts[0](head)
        value = first
        for share, part in zip(shares, parts[1:]):
            value = value + share[:, head : head + 1] * (part(head) - first)
        return value

    return head_of, best + jnp.log(total)


def part_of(ref, start, rows):
    return lambda head: ref[:, head * HD : (head + 1) * HD].astype(f32)[start : start + rows]


def top_of(ref, start, rows):
    return join_top(ref[:, ref.shape[1] - LANES :].astype(f32)[start : start + rows])


def merge_kernel(count, *refs):
    ins, outs = refs[:count], refs[count:]
    heads = ins[0].shape[1] // HD - 1
    rows = sum(out.shape[0] for out in outs)
    head_of, top = merge(
        [part_of(ref, 0, rows) for ref in ins], [top_of(ref, 0, rows) for ref in ins]
    )
    for head in range(heads + 1):
        cut = slice(head * HD, (head + 1) * HD)
        block = head_of(head) if head < heads else split_top(top)
        at = 0
        for out in outs:
            out[:, cut] = block[at : at + out.shape[0]].astype(bf16)
            at += out.shape[0]


def early_kernel(count, *refs):
    ins = refs[:count]
    new_values, own_top, out = refs[count:]
    rows = out.shape[0]
    heads = new_values.shape[1] // HD
    head_of, top = merge(
        [part_of(ref, ref.shape[0] - rows, rows) for ref in ins] + [part_of(new_values, 0, rows)],
        [top_of(ref, ref.shape[0] - rows, rows) for ref in ins] + [own_top[...]],
    )
    for head in range(heads):
        out[:, head * HD : (head + 1) * HD] = head_of(head)
    out[:, heads * HD :] = top


def last_kernel(count, *refs):
    ins, early, out = refs[:count], refs[count], refs[count + 1]
    rows, width = out.shape
    head_of, _ = merge(
        [part_of(early, 0, rows)] + [part_of(ref, 0, rows) for ref in ins],
        [early[:, width:]] + [top_of(ref, 0, rows) for ref in ins],
    )
    for head in range(width // HD):
        out[:, head * HD : (head + 1) * HD] = head_of(head).astype(bf16)


def project_kernel(mid, own_rows, count, *refs):
    blocks, weight, outs, acc = refs[:count], refs[count], refs[count + 1 : -1], refs[-1]
    product = lax.dot_general(
        stacked(blocks).astype(bf16),
        weight[...],
        (((1,), (1,)), ((), ())),
        preferred_element_type=f32,
    )
    for at, distance in enumerate(gather_order(mid, RESULT_ORDER)):
        owner = lax.bitwise_xor(lax.axis_index("kv"), distance)
        start = pl.multiple_of(owner * own_rows, own_rows)
        acc[pl.ds(start, own_rows), :] = product[at * own_rows : (at + 1) * own_rows]
    for distance, out in enumerate(outs):
        rows = out.shape[0]
        side = lax.bitwise_xor(lax.axis_index("tp"), distance)
        out[...] = acc[pl.ds(pl.multiple_of(side * rows, rows), rows), :].astype(out.dtype)


def base_kernel(kept, residual, bias, total):
    total[...] = kept[...] + residual[...].astype(f32) + bias[...].astype(f32)


def final_kernel(total, *refs):
    value = total[...]
    for part in refs[:-1]:
        value = value + part[...].astype(f32)
    refs[-1][...] = value.astype(bf16)


def hop(x, axis, count, distance):
    return lax.ppermute(x, axis, [(i, i ^ distance) for i in range(count)])


def on_device(
    kv_count,
    tp_count,
    queries,
    new_keys,
    new_values,
    keys,
    values,
    slot_request,
    slot_valid,
    out_weight,
    out_bias,
    residual,
):
    own_rows, width = queries.shape
    slots = keys.shape[0]
    mid = kv_count // (2 * OUTER)
    requests = kv_count * own_rows
    rows = slots // PAGE
    wide = width + LANES
    kv_hop = lambda x, distance: hop(x, "kv", kv_count, distance)
    shaped = jax.ShapeDtypeStruct

    def call(kernel, shapes, scratch, name, *operands, spec=lambda at: WHOLE):
        single = not isinstance(shapes, tuple)
        return pl.pallas_call(
            kernel,
            out_shape=shapes,
            in_specs=[spec(at) for at in range(len(operands))],
            out_specs=WHOLE if single else (WHOLE,) * len(shapes),
            scratch_shapes=scratch,
            compiler_params=params(),
            name=name,
        )(*operands)

    def pack(parts, *after):
        return call(
            functools.partial(pack_kernel, len(parts)),
            shaped((sum(x.shape[0] for x in parts), width), bf16),
            [],
            "pack",
            *parts,
            *after,
            spec=lambda at: WHOLE if at < len(parts) else ANY,
        )

    def gather(block, own, order, before, after, beside):
        outer = {far: kv_hop(block, 2 * mid * far) for far in order}
        across = [
            kv_hop(block, 2 * middle + 2 * mid * order[2]) for middle in range(1, mid)
        ]
        relay = pack([outer[far] for far in relayed(order)] + [own], *before)
        near = pack([relay, outer[order[2]], *across], *beside)
        far = [kv_hop(relay, 2 * middle) for middle in range(1, mid)]
        if after:
            far = [pack(far, *after)]
        line = [near] + far
        return line + [kv_hop(x, 1) for x in line]

    pick, spread_to, mask = call(
        functools.partial(prep_kernel, mid, own_rows),
        (
            shaped((rows, requests), bf16),
            shaped((rows, requests), bf16),
            shaped((rows, slots), f32),
        ),
        [],
        "prep",
        slot_request.reshape(1, slots),
        slot_valid.reshape(1, slots),
    )
    held = call(hold_kernel, shaped(queries.shape, bf16), [], "hold", queries)
    own_top = call(own_kernel, shaped((own_rows, LANES), f32), [], "own", held, new_keys)
    ready = [
        call(ready_kernel, shaped((8, LANES), f32), [], "ready", x, spec=lambda at: ANY)
        for x in (keys, values)
    ]
    blocks = gather(queries, held, QUERY_ORDER, [own_top], [ready[0], pick], [ready[1]])
    size = OUTER * own_rows
    outs = call(
        functools.partial(attend_kernel, len(blocks)),
        (shaped((size, wide), bf16),) * (2 * mid),
        [],
        "attend",
        pick,
        spread_to,
        mask,
        keys,
        values,
        *blocks,
    )

    def merged(ins, *heights):
        return call(
            functools.partial(merge_kernel, len(ins)),
            tuple(shaped((height * own_rows, wide), bf16) for height in heights),
            [],
            "merge",
            *ins,
        )

    relays, ins = [], []
    for middle in range(1, mid):
        relay, straight = merged([outs[middle], kv_hop(outs[mid + middle], 1)], 3, 1)
        relays.append(kv_hop(relay, 2 * middle))
        ins.append(kv_hop(straight, 2 * middle + 2 * mid * REDUCE_ORDER[2]))
    *pair, own, straight = merged([outs[0], kv_hop(outs[mid], 1)], 2, 1, 1)
    pair = merged(pair + relays, 1, 1)
    ins += [own, *relays, kv_hop(straight, 2 * mid * REDUCE_ORDER[2])]
    early = call(
        functools.partial(early_kernel, len(ins)),
        shaped((own_rows, wide), f32),
        [],
        "early",
        *ins,
        new_values,
        own_top,
    )
    ins = [kv_hop(x, 2 * mid * far) for x, far in zip(pair, relayed(REDUCE_ORDER))]
    attended = call(
        functools.partial(last_kernel, len(ins)),
        shaped((own_rows, width), bf16),
        [],
        "last",
        *ins,
        early,
    )

    blocks = gather(attended, attended, RESULT_ORDER, [], [], [])
    columns = out_weight.shape[1]
    shape = (requests // tp_count, columns)
    kept, *sent = call(
        functools.partial(project_kernel, mid, own_rows, len(blocks)),
        (shaped(shape, f32),) + (shaped(shape, SENT),) * (tp_count - 1),
        [pltpu.VMEM((requests, columns), f32)],
        "project",
        *blocks,
        out_weight.T,
    )
    received = [hop(x, "tp", tp_count, at + 1) for at, x in enumerate(sent)]
    total = call(
        base_kernel, shaped(shape, f32), [], "base", kept, residual, out_bias.reshape(1, columns)
    )
    return call(final_kernel, shaped(shape, bf16), [], "final", total, *received)


def solution(mesh):
    placed = (
        P("kv", "tp"),
        P("kv", "tp"),
        P("kv", "tp"),
        P("kv", "tp"),
        P("kv", "tp"),
        P("kv"),
        P("kv"),
        P("tp", "kv"),
        P("kv"),
        P("tp", "kv"),
    )
    return jax.shard_map(
        functools.partial(on_device, mesh.shape["kv"], mesh.shape["tp"]),
        mesh=mesh,
        in_specs=placed,
        out_specs=P("tp", "kv"),
        check_vma=False,
    )
```
